256 devices in a mesh: pre: 8 (over z), req: 32 (over x, y, core).
Axes of the slice: x: 4, y: 4, z: 8, core: 2. Of those that a mesh axis runs over, the one named last changes fastest.
Arguments:
- queries: bfloat16 [32, 16384], P('req', 'pre'), may hold values from -120 to 120
- prefix_keys: bfloat16 [131072, 1024], P(('pre', 'req')), may hold values from -4.6 to 4.6
- prefix_values: bfloat16 [131072, 1024], P(('pre', 'req')), may hold values from -6 to 6
- suffix_keys: bfloat16 [32, 2048, 1024], P('req', 'pre'), may hold values from -8 to 8
- suffix_values: bfloat16 [32, 2048, 1024], P('req', 'pre'), may hold values from -6 to 6
- suffix_lengths: int32 [32], P('req'), may hold values from 1 to 2048, 32768 in all
Outputs:
- attention: bfloat16 [32, 16384], P('req', 'pre')
The draws below stay inside these ranges and needn't reach their ends.
All inputs are finite; a program needn't handle non-finite values. No bound on the sum of `suffix_lengths` on one device may be relied on, other than what follows from the above.
Results may differ from the reference program's by a relative error of at most 0.0055.
Values may be sent and summed in bfloat16 or wider, within the bound.
A program may use at most 64 MiB of HBM per device.

```python
import math
import jax
import jax.numpy as jnp
import numpy as np
from jax import lax

H = 128
KVH = 8
DH = 128
PRE_DEV = 512
REQS = 32
PREFIX = 131072
SUF = 2048
N_PRE = 8
N_REQ = 32


def prefix_table(key, row_ids):
    base_key = jax.random.fold_in(key, 7)

    def one_row(row_id):
        sampled = jax.random.normal(jax.random.fold_in(base_key, row_id), (KVH * DH,), jnp.float32)
        return jnp.clip(sampled, -4.5, 4.5)
    return jax.vmap(one_row)(row_ids)


def draw_prefix_keys(key, part):
    key_table = prefix_table(key, jnp.arange(PREFIX, dtype=jnp.int32))
    return key_table.astype(jnp.bfloat16)


def draw_queries(key, part):
    own_key = jax.random.fold_in(key, 3)
    sampled = 3.0 * jnp.clip(jax.random.normal(own_key, (REQS, H * DH), jnp.float32), -6.0, 6.0)
    return sampled.astype(jnp.bfloat16)


def shard_levels(key, dims, cuts, low, top_value):
    factor_of = 1.0
    for dim, blocks in cuts:
        draws = jax.random.uniform(jax.random.fold_in(jax.random.fold_in(key, 6), dim), (blocks,), jnp.float32, low / len(cuts), top_value / len(cuts))
        factor_of = factor_of * jnp.repeat(jnp.exp(draws), dims[dim] // blocks).reshape((-1,) + (1,) * (len(dims) - 1 - dim))
    return factor_of


def length_profile(number_of, total, bound, slope):
    portions = [(1 << 20) // math.isqrt(standing ** slope) + 1 for standing in range(2, number_of + 1)]
    rest, given = total - bound - (number_of - 1), [1] * (number_of - 1)
    while rest > 0:
        free = [i for i in range(number_of - 1) if given[i] < bound]
        mass, budget = sum([portions[i] for i in free]), rest
        for i in free:
            addition = min(bound - given[i], max(1, budget * portions[i] // mass), rest)
            given[i] = given[i] + addition
            rest = rest - addition
    return np.array([bound] + given)


def ragged(key, count, total, limit, lean):
    if count == 2:
        one = jax.random.randint(key, (), max(1, total - limit), min(limit, total - 1) + 1)
        return jnp.stack([one, total - one])
    lengths = jnp.asarray(length_profile(count, total, limit, lean), jnp.int32)
    pairs = (count - 1) // 2
    donor, sink = lengths[1:1 + 2 * pairs:2], lengths[2:2 + 2 * pairs:2]
    slack = jnp.minimum(donor - 1, limit - sink)
    shifted = jax.random.randint(jax.random.fold_in(key, 1), (pairs,), 0, 1 << 20) % (slack + 1)
    lengths = lengths.at[1:1 + 2 * pairs:2].set(donor - shifted).at[2:2 + 2 * pairs:2].set(sink + shifted)
    return lengths[jax.random.permutation(jax.random.fold_in(key, 2), count)]


def scatter_about(stream_key, extent, deviation, most, cuts=(), kind=jnp.bfloat16):
    values = jax.random.normal(stream_key, extent, jnp.float32) * deviation
    if len(cuts) > 0:
        values = shard_levels(stream_key, extent, cuts, -0.22, 0.18) * values
    return jnp.clip(values, min=-most, max=most).astype(kind)


def setup_inputs(seed: int = 0) -> dict:
    key_list = jax.random.split(jax.random.key(seed), 7)
    return {
        "queries": draw_queries(jax.random.fold_in(key_list[6], 71), 0),
        "prefix_keys": draw_prefix_keys(jax.random.fold_in(key_list[6], 71), 0),
        "prefix_values": scatter_about(key_list[2], (PREFIX, KVH * DH), 1.0, 6.0, ((0, 256),)),
        "suffix_keys": scatter_about(key_list[3], (REQS, SUF, KVH * DH), 1.4, 8.0, ((0, 32), (1, 8))),
        "suffix_values": scatter_about(key_list[4], (REQS, SUF, KVH * DH), 1.0, 6.0, ((0, 32), (1, 8))),
        "suffix_lengths": ragged(key_list[5], REQS, REQS * SUF // 2, SUF, 1).astype(jnp.int32),
    }


def rounded_copy(values):
    lowered = values.astype(jnp.bfloat16)
    lowered = lax.optimization_barrier(lowered)
    return lowered.astype(jnp.float32)

def reference(queries, prefix_keys, prefix_values, suffix_keys, suffix_values, suffix_lengths):
    softmax_scale = 1.0 / math.sqrt(DH)
    per_group = H // KVH
    query_grid = queries.astype(jnp.float32).reshape(REQS, KVH, per_group, DH)
    block_rows = PRE_DEV * N_PRE
    block_ids = jnp.arange(N_REQ, dtype=jnp.int32)

    def block_scores(block_index):
        start = (block_index * block_rows).astype(jnp.int32)
        key_block = lax.dynamic_slice_in_dim(prefix_keys, start, block_rows, 0).astype(jnp.float32)
        key_block = key_block.reshape(block_rows, KVH, DH)
        return jnp.einsum('rghd,bgd->rghb', query_grid, key_block, precision=lax.Precision.HIGHEST) * softmax_scale
    prefix_peak = lax.optimization_barrier(jnp.max(lax.map(lambda block_index: lax.optimization_barrier(jnp.max(block_scores(block_index), axis=-1)), block_ids), axis=0))
    suffix_grid = suffix_keys.astype(jnp.float32).reshape(REQS, SUF, KVH, DH)
    suffix_scores = jnp.einsum('rghd,rsgd->rghs', query_grid, suffix_grid, precision=lax.Precision.HIGHEST) * softmax_scale
    visible = (jnp.arange(SUF, dtype=jnp.int32)[None, :] < suffix_lengths[:, None])[:, None, None, :]
    masked = jnp.where(visible, suffix_scores, -jnp.inf)
    peak = jnp.maximum(prefix_peak, lax.optimization_barrier(jnp.max(masked, axis=-1)))

    def accumulate(totals, block_index):
        numerator, denominator = totals
        weights = rounded_copy(jnp.exp(block_scores(block_index) - peak[..., None]))
        start = (block_index * block_rows).astype(jnp.int32)
        value_block = lax.dynamic_slice_in_dim(prefix_values, start, block_rows, 0).astype(jnp.float32)
        value_block = value_block.reshape(block_rows, KVH, DH)
        numerator = numerator + jnp.einsum('rghb,bgd->rghd', weights, value_block, precision=lax.Precision.HIGHEST)
        denominator = denominator + lax.optimization_barrier(jnp.sum(weights, axis=-1))
        return ((numerator, denominator), None)
    start_totals = (jnp.zeros((REQS, KVH, per_group, DH), jnp.float32), jnp.zeros((REQS, KVH, per_group), jnp.float32))
    (numerator, denominator), unused = lax.scan(accumulate, start_totals, block_ids)
    suffix_weights = rounded_copy(jnp.exp(masked - peak[..., None]))
    value_grid = suffix_values.astype(jnp.float32).reshape(REQS, SUF, KVH, DH)
    numerator = numerator + jnp.einsum('rghs,rsgd->rghd', suffix_weights, value_grid, precision=lax.Precision.HIGHEST)
    denominator = denominator + lax.optimization_barrier(jnp.sum(suffix_weights, axis=-1))
    result = numerator / denominator[..., None]
    return result.reshape(REQS, H * DH).astype(jnp.bfloat16)
```

```python
import functools
import math

import jax
import jax.numpy as jnp
from jax import lax
from jax.experimental import pallas as pl
from jax.experimental.pallas import tpu as pltpu
from jax.sharding import PartitionSpec as P

MESH = pl.DeviceIdType.MESH
DH = 128
HG = 16
F32 = jnp.float32
BF16 = jnp.bfloat16
SCALE = math.log2(math.e) / math.sqrt(DH)
NEG = -1e30


def kernel(
    dims, pieces, row_chunks,
    q_ref, k_ref, v_ref, sk_ref, sv_ref, len_ref, out_ref,
    kb, vx, skb, svb, qz, qa, ob, ib, zo, zi, sn, sml,
    local_sem, kv_sem, z_sem, qs_sem, qr_sem, os_sem, or_sem, zz_sem,
):
    npre, nx, ny = dims
    nreq = nx * ny * 2
    half = npre // 2
    tokens = k_ref.shape[0]
    slots = sk_ref.shape[1]
    per_piece = half // pieces
    p = lax.axis_index("pre")
    r = lax.axis_index("req")
    c = r % 2
    x = r // (2 * ny)
    y = (r // 2) % ny
    other = 1 - c
    sib = r + 1 - 2 * c

    def mate(k):
        kc = k % 2
        ky = (k // 2) % ny
        kx = k // (2 * ny)
        return (((x + kx) % nx) * ny + (y + ky) % ny) * 2 + (c + kc) % 2

    def columns(core, g):
        return pl.ds(pl.multiple_of((half * core + g) * DH, DH), DH)

    def own_rows():
        return pl.ds(pl.multiple_of(c * tokens, tokens), tokens)

    local = []
    for g in range(half):
        local.append(pltpu.make_async_copy(k_ref.at[:, columns(c, g)], kb.at[g, own_rows(), :], local_sem.at[0]))
        local.append(
            pltpu.make_async_copy(v_ref.at[:, columns(c, g)], vx.at[g, own_rows(), pl.ds(0, DH)], local_sem.at[1])
        )
    suffix = [
        pltpu.make_async_copy(sk_ref.at[0], skb, local_sem.at[2]),
        pltpu.make_async_copy(sv_ref.at[0], svb, local_sem.at[3]),
    ]
    for copy in local + suffix:
        copy.start()

    barrier = pltpu.get_barrier_semaphore()

    def greet_pre(k, carry):
        pl.semaphore_signal(barrier, inc=1, device_id=((p + k) % npre, r), device_id_type=MESH)
        return carry

    def greet_req(k, carry):
        pl.semaphore_signal(barrier, inc=1, device_id=(p, mate(k)), device_id_type=MESH)
        return carry

    lax.fori_loop(1, npre, greet_pre, 0)
    lax.fori_loop(1, nreq, greet_req, 0)

    tile = jnp.concatenate([q_ref[:, h * DH : (h + 1) * DH].astype(F32) for h in range(HG)], axis=0)
    qz[p] = tile.astype(BF16)
    pl.semaphore_wait(barrier, npre - 1 + nreq - 1)

    def z_copy(k):
        return pltpu.make_async_remote_copy(
            src_ref=qz.at[p], dst_ref=qz.at[p], send_sem=z_sem.at[0], recv_sem=z_sem.at[1],
            device_id=((p + k) % npre, r), device_id_type=MESH,
        )

    def z_send(k, carry):
        z_copy(k).start()
        return carry

    lax.fori_loop(1, npre, z_send, 0)

    swaps = []
    for g in range(half):
        swaps.append((k_ref.at[:, columns(other, g)], kb.at[g, own_rows(), :], 0))
        swaps.append((v_ref.at[:, columns(other, g)], vx.at[g, own_rows(), pl.ds(0, DH)], 1))
    swaps = [
        pltpu.make_async_remote_copy(
            src_ref=src, dst_ref=dst, send_sem=kv_sem.at[i], recv_sem=kv_sem.at[2 + i],
            device_id=(p, sib), device_id_type=MESH,
        )
        for src, dst, i in swaps
    ]
    for copy in swaps:
        copy.start()

    def fill(g, carry):
        vx[g, :, DH : 2 * DH] = jnp.ones((2 * tokens, DH), BF16)
        ob[:, half] = jnp.zeros((nreq, HG, DH), BF16)
        return carry

    lax.fori_loop(0, half, fill, 0)

    def drain(ref, sem):
        pltpu.make_async_copy(ref, ref, sem).wait()

    drain(qz.at[pl.ds(0, npre - 1)], z_sem.at[1])

    def q_send(k, carry):
        target = mate(k)
        for j in range(pieces):
            pltpu.make_async_remote_copy(
                src_ref=qz.at[pl.ds(half * (target % 2) + j * per_piece, per_piece)],
                dst_ref=qa.at[r, pl.ds(j * per_piece, per_piece)],
                send_sem=qs_sem.at[0], recv_sem=qr_sem.at[j],
                device_id=(p, target), device_id_type=MESH,
            ).start()
        return carry

    lax.fori_loop(1, nreq, q_send, 0)
    qa[r] = qz[pl.ds(half * c, half)]

    for copy in suffix:
        copy.wait()
    visible = (p * slots + lax.broadcasted_iota(jnp.int32, (HG, slots), 1)) < len_ref[0]
    for g in range(npre):
        s = lax.dot_general(
            qz[g], skb[:, g * DH : (g + 1) * DH], (((1,), (1,)), ((), ())), preferred_element_type=F32
        )
        s = jnp.where(visible, s * SCALE, NEG)
        m = jnp.max(s, axis=1, keepdims=True).astype(BF16).astype(F32)
        w = jnp.where(visible, jnp.exp2(s - m), 0.0).astype(BF16)
        sn[g] = jnp.dot(w, svb[:, g * DH : (g + 1) * DH], preferred_element_type=F32)
        l = jnp.sum(w.astype(F32), axis=1, keepdims=True)
        sml[g, 0] = jnp.broadcast_to(m, (HG, DH))
        sml[g, 1] = jnp.broadcast_to(l, (HG, DH))

    keys, values = kb.at[:, pl.ds(0, tokens), :], vx.at[:, pl.ds(0, tokens), pl.ds(0, DH)]
    drain(keys, local_sem.at[0])
    drain(values, local_sem.at[1])
    drain(keys, kv_sem.at[2])
    drain(values, kv_sem.at[3])

    chunk = nreq // row_chunks
    lane = lax.broadcasted_iota(jnp.int32, (chunk * HG, DH), 1)

    def piece_step(j, carry):
        drain(qa.at[pl.ds(0, nreq - 1), pl.ds(0, per_piece)], qr_sem.at[j])

        def group_step(i, carry):
            g = j * per_piece + i
            for ch in range(row_chunks):
                rows = pl.ds(ch * chunk, chunk)
                qc = qa[rows, g].reshape(chunk * HG, DH)
                s = lax.dot_general(qc, kb[g], (((1,), (1,)), ((), ())), preferred_element_type=F32)
                m = (jnp.max(s, axis=1, keepdims=True) * SCALE).astype(BF16).astype(F32)
                w = jnp.exp2(s * SCALE - m).astype(BF16)
                o = jnp.dot(w, vx[g], preferred_element_type=F32)
                ob[rows, g] = o[:, :DH].astype(BF16).reshape(chunk, HG, DH)
                l = o[:, DH:]
                high = l.astype(BF16).astype(F32)
                stats = ob[rows, half].reshape(chunk * HG, DH).astype(F32)
                stats = jnp.where(lane == 4 * g, m, stats)
                stats = jnp.where(lane == 4 * g + 1, high, stats)
                stats = jnp.where(lane == 4 * g + 2, l - high, stats)
                ob[rows, half] = stats.astype(BF16).reshape(chunk, HG, DH)
            return carry

        lax.fori_loop(0, per_piece, group_step, 0)

        def o_send(k, carry):
            target = mate(k)
            span = pl.ds(j * per_piece, per_piece)
            pltpu.make_async_remote_copy(
                src_ref=ob.at[target, span], dst_ref=ib.at[r, span],
                send_sem=os_sem.at[0], recv_sem=or_sem.at[0],
                device_id=(p, target), device_id_type=MESH,
            ).start()
            return carry

        lax.fori_loop(1, nreq, o_send, 0)
        return carry

    lax.fori_loop(0, pieces, piece_step, 0)

    def stat_send(k, carry):
        target = mate(k)
        pltpu.make_async_remote_copy(
            src_ref=ob.at[target, half], dst_ref=ib.at[r, half],
            send_sem=os_sem.at[0], recv_sem=or_sem.at[0],
            device_id=(p, target), device_id_type=MESH,
        ).start()
        return carry

    lax.fori_loop(1, nreq, stat_send, 0)
    ib[r] = ob[r]
    drain(ib.at[pl.ds(0, nreq - 1)], or_sem.at[0])

    chips = nx * ny
    small = lax.broadcasted_iota(jnp.int32, (HG, DH), 1)
    for core in range(2):
        stat = [ib[2 * i + core, half].astype(F32) for i in range(chips)]
        top = functools.reduce(jnp.maximum, stat)
        factor = [jnp.exp2(t - top) for t in stat]
        total = functools.reduce(
            jnp.add,
            [t * pltpu.roll(f, 1, 1) for t, f in zip(stat, factor)],
        )
        rest = functools.reduce(jnp.add, [t * pltpu.roll(f, 2, 1) for t, f in zip(stat, factor)])
        for i in range(half):
            g = half * core + i
            num = functools.reduce(
                jnp.add,
                [f[:, 4 * i : 4 * i + 1] * ib[2 * n + core, i].astype(F32) for n, f in enumerate(factor)],
            )
            peak = top[:, 4 * i : 4 * i + 1]
            l = total[:, 4 * i + 1 : 4 * i + 2] + rest[:, 4 * i + 2 : 4 * i + 3]
            sm = sml[g, 0]
            both = jnp.maximum(sm, peak)
            fp = jnp.exp2(peak - both)
            fs = jnp.exp2(sm - both)
            num = num * fp + sn[g] * fs
            l = l * fp + sml[g, 1] * fs
            high = l.astype(BF16).astype(F32)
            zo[g, 0] = num.astype(BF16)
            zo[g, 1] = jnp.where(small == 0, both, jnp.where(small == 1, high, l - high)).astype(BF16)

    def zz_send(k, carry):
        target = (p + k) % npre
        pltpu.make_async_remote_copy(
            src_ref=zo.at[target], dst_ref=zi.at[p], send_sem=zz_sem.at[0], recv_sem=zz_sem.at[1],
            device_id=(target, r), device_id_type=MESH,
        ).start()
        return carry

    lax.fori_loop(1, npre, zz_send, 0)
    zi[p] = zo[p]
    drain(zi.at[pl.ds(0, npre - 1)], zz_sem.at[1])
    stat = [zi[i, 1].astype(F32) for i in range(npre)]
    peaks = [t[:, 0:1] for t in stat]
    top = functools.reduce(jnp.maximum, peaks)
    factor = [jnp.exp2(t - top) for t in peaks]
    num = functools.reduce(jnp.add, [f * zi[i, 0].astype(F32) for i, f in enumerate(factor)])
    l = functools.reduce(jnp.add, [f * (t[:, 1:2] + t[:, 2:3]) for f, t in zip(factor, stat)])
    out_ref[...] = num / l

    drain(qz.at[pl.ds(0, npre - 1)], z_sem.at[0])
    drain(keys, kv_sem.at[0])
    drain(values, kv_sem.at[1])
    drain(qa.at[pl.ds(0, nreq - 1)], qs_sem.at[0])
    drain(ib.at[pl.ds(0, nreq - 1)], os_sem.at[0])
    drain(zi.at[pl.ds(0, npre - 1)], zz_sem.at[0])


def on_device(dims, pieces, row_chunks, queries, prefix_keys, prefix_values, suffix_keys, suffix_values, suffix_lengths):
    npre, nx, ny = dims
    nreq = nx * ny * 2
    half = npre // 2
    tokens = prefix_keys.shape[0]
    slots = suffix_keys.shape[1]
    width = npre * DH
    vmem = pl.BlockSpec(memory_space=pltpu.VMEM)
    hbm = pl.BlockSpec(memory_space=pl.ANY)
    dma = pltpu.SemaphoreType.DMA
    out = pl.pallas_call(
        functools.partial(kernel, dims, pieces, row_chunks),
        out_shape=jax.ShapeDtypeStruct((HG, DH), F32),
        in_specs=[vmem, hbm, hbm, hbm, hbm, pl.BlockSpec(memory_space=pltpu.SMEM)],
        out_specs=vmem,
        scratch_shapes=[
            pltpu.VMEM((half, 2 * tokens, DH), BF16),
            pltpu.VMEM((half, 2 * tokens, 2 * DH), BF16),
            pltpu.VMEM((slots, width), BF16),
            pltpu.VMEM((slots, width), BF16),
            pltpu.VMEM((npre, HG, DH), BF16),
            pltpu.VMEM((nreq, half, HG, DH), BF16),
            pltpu.VMEM((nreq, half + 1, HG, DH), BF16),
            pltpu.VMEM((nreq, half + 1, HG, DH), BF16),
            pltpu.VMEM((npre, 2, HG, DH), BF16),
            pltpu.VMEM((npre, 2, HG, DH), BF16),
            pltpu.VMEM((npre, HG, DH), F32),
            pltpu.VMEM((npre, 2, HG, DH), F32),
            dma((4,)),
            dma((4,)),
            dma((2,)),
            dma((1,)),
            dma((pieces,)),
            dma((1,)),
            dma((1,)),
            dma((2,)),
        ],
        compiler_params=pltpu.CompilerParams(
            collective_id=0, has_side_effects=True, vmem_limit_bytes=32 * 1024 * 1024
        ),
    )(queries, prefix_keys, prefix_values, suffix_keys, suffix_values, suffix_lengths)
    return out.astype(BF16).reshape(1, HG * DH)


def build(mesh, dims, pieces, row_chunks):
    placed = (
        P("req", "pre"),
        P(("pre", "req"), None),
        P(("pre", "req"), None),
        P("req", "pre", None),
        P("req", "pre", None),
        P("req"),
    )
    return jax.shard_map(
        functools.partial(on_device, dims, pieces, row_chunks),
        mesh=mesh, in_specs=placed, out_specs=P("req", "pre"), check_vma=False,
    )


def solution(mesh):
    return build(mesh, (8, 4, 4), 4, 4)
```

```python
import functools
import math

import jax
import jax.numpy as jnp
from jax import lax
from jax.experimental import pallas as pl
from jax.experimental.pallas import tpu as pltpu
from jax.sharding import PartitionSpec as P

MESH = pl.DeviceIdType.MESH
DH = 128
HG = 16
F32 = jnp.float32
BF16 = jnp.bfloat16
SCALE = math.log2(math.e) / math.sqrt(DH)
NEG = -1e30


def plane_offsets(nx, ny):
    def hops(o):
        return min(o[0], nx - o[0]) + min(o[1], ny - o[1])

    offsets = [(i, j, k) for i in range(nx) for j in range(ny) for k in range(2)]
    offsets.sort(key=lambda o: (-hops(o), o == (0, 0, 0)))
    back = [offsets.index(((-i) % nx, (-j) % ny, k)) for i, j, k in offsets]
    return offsets, back


def kernel(
    dims, pieces, row_chunks,
    q_ref, k_ref, v_ref, sk_ref, sv_ref, len_ref, out_ref,
    kb, vx, skb, svb, qz, qa, ob, ib, zo, zi, sn, sml,
    local_sem, kv_sem, z_sem, qs_sem, qr_sem, os_sem, or_sem, zz_sem,
):
    npre, nx, ny = dims
    nreq = nx * ny * 2
    half = npre // 2
    tokens = k_ref.shape[0]
    slots = sk_ref.shape[1]
    per_piece = half // pieces
    p = lax.axis_index("pre")
    r = lax.axis_index("req")
    c = r % 2
    x = r // (2 * ny)
    y = (r // 2) % ny
    other = 1 - c
    sib = r + 1 - 2 * c

    offsets, back = plane_offsets(nx, ny)
    own = nreq - 1

    def mate(k):
        kx, ky, kc = offsets[k]
        return (((x + kx) % nx) * ny + (y + ky) % ny) * 2 + (c + kc) % 2

    def pre_mate(k):
        return (p + k) % npre

    def columns(core, g):
        return pl.ds(pl.multiple_of((half * core + g) * DH, DH), DH)

    def own_rows():
        return pl.ds(pl.multiple_of(c * tokens, tokens), tokens)

    local = []
    for g in range(half):
        local.append(pltpu.make_async_copy(k_ref.at[:, columns(c, g)], kb.at[g, own_rows(), :], local_sem.at[0]))
        local.append(
            pltpu.make_async_copy(v_ref.at[:, columns(c, g)], vx.at[g, own_rows(), pl.ds(0, DH)], local_sem.at[1])
        )
    suffix = [
        pltpu.make_async_copy(sk_ref.at[0], skb, local_sem.at[2]),
        pltpu.make_async_copy(sv_ref.at[0], svb, local_sem.at[3]),
    ]
    for copy in local + suffix:
        copy.start()

    barrier = pltpu.get_barrier_semaphore()

    for k in range(1, npre):
        pl.semaphore_signal(barrier, inc=1, device_id=(pre_mate(k), r), device_id_type=MESH)
    for k in range(own):
        pl.semaphore_signal(barrier, inc=1, device_id=(p, mate(k)), device_id_type=MESH)

    tile = jnp.concatenate([q_ref[:, h * DH : (h + 1) * DH].astype(F32) for h in range(HG)], axis=0)
    qz[p] = tile.astype(BF16)
    pl.semaphore_wait(barrier, npre - 1 + nreq - 1)

    far_first = sorted(range(1, npre), key=lambda k: -min(k, npre - k))
    for k in far_first:
        pltpu.make_async_remote_copy(
            src_ref=qz.at[p], dst_ref=qz.at[p], send_sem=z_sem.at[0], recv_sem=z_sem.at[1],
            device_id=(pre_mate(k), r), device_id_type=MESH,
        ).start()

    swaps = []
    for g in range(half):
        swaps.append((k_ref.at[:, columns(other, g)], kb.at[g, own_rows(), :], 0))
        swaps.append((v_ref.at[:, columns(other, g)], vx.at[g, own_rows(), pl.ds(0, DH)], 1))
    swaps = [
        pltpu.make_async_remote_copy(
            src_ref=src, dst_ref=dst, send_sem=kv_sem.at[i], recv_sem=kv_sem.at[2 + i],
            device_id=(p, sib), device_id_type=MESH,
        )
        for src, dst, i in swaps
    ]
    for copy in swaps:
        copy.start()

    def fill(g, carry):
        vx[g, :, DH : 2 * DH] = jnp.ones((2 * tokens, DH), BF16)
        ob[:, half] = jnp.zeros((nreq, HG, DH), BF16)
        return carry

    lax.fori_loop(0, half, fill, 0)

    def drain(ref, sem):
        pltpu.make_async_copy(ref, ref, sem).wait()

    drain(qz.at[pl.ds(0, npre - 1)], z_sem.at[1])

    def q_send(j, carry):
        span = pl.ds(j * per_piece, per_piece)
        for k in range(own):
            core = (c + offsets[k][2]) % 2
            pltpu.make_async_remote_copy(
                src_ref=qz.at[pl.ds(half * core + j * per_piece, per_piece)],
                dst_ref=qa.at[back[k], span],
                send_sem=qs_sem.at[0], recv_sem=qr_sem.at[j],
                device_id=(p, mate(k)), device_id_type=MESH,
            ).start()
        return carry

    lax.fori_loop(0, pieces, q_send, 0)
    qa[own] = qz[pl.ds(half * c, half)]

    for copy in suffix:
        copy.wait()
    visible = (p * slots + lax.broadcasted_iota(jnp.int32, (HG, slots), 1)) < len_ref[0]
    for g in range(npre):
        s = lax.dot_general(
            qz[g], skb[:, g * DH : (g + 1) * DH], (((1,), (1,)), ((), ())), preferred_element_type=F32
        )
        s = jnp.where(visible, s * SCALE, NEG)
        m = jnp.max(s, axis=1, keepdims=True).astype(BF16).astype(F32)
        w = jnp.where(visible, jnp.exp2(s - m), 0.0).astype(BF16)
        sn[g] = jnp.dot(w, svb[:, g * DH : (g + 1) * DH], preferred_element_type=F32)
        l = jnp.sum(w.astype(F32), axis=1, keepdims=True)
        sml[g, 0] = jnp.broadcast_to(m, (HG, DH))
        sml[g, 1] = jnp.broadcast_to(l, (HG, DH))

    keys, values = kb.at[:, pl.ds(0, tokens), :], vx.at[:, pl.ds(0, tokens), pl.ds(0, DH)]
    drain(keys, local_sem.at[0])
    drain(values, local_sem.at[1])
    drain(keys, kv_sem.at[2])
    drain(values, kv_sem.at[3])

    chunk = nreq // row_chunks
    lane = lax.broadcasted_iota(jnp.int32, (chunk * HG, DH), 1)

    def piece_step(j, carry):
        drain(qa.at[pl.ds(0, own), pl.ds(0, per_piece)], qr_sem.at[j])

        def group_step(i, carry):
            g = j * per_piece + i
            for ch in range(row_chunks):
                rows = pl.ds(ch * chunk, chunk)
                qc = qa[rows, g].reshape(chunk * HG, DH)
                s = lax.dot_general(qc, kb[g], (((1,), (1,)), ((), ())), preferred_element_type=F32)
                m = (jnp.max(s, axis=1, keepdims=True) * SCALE).astype(BF16).astype(F32)
                w = jnp.exp2(s * SCALE - m).astype(BF16)
                o = jnp.dot(w, vx[g], preferred_element_type=F32)
                ob[rows, g] = o[:, :DH].astype(BF16).reshape(chunk, HG, DH)
                l = o[:, DH:]
                high = l.astype(BF16).astype(F32)
                stats = ob[rows, half].reshape(chunk * HG, DH).astype(F32)
                stats = jnp.where(lane == 4 * g, m, stats)
                stats = jnp.where(lane == 4 * g + 1, high, stats)
                stats = jnp.where(lane == 4 * g + 2, l - high, stats)
                ob[rows, half] = stats.astype(BF16).reshape(chunk, HG, DH)
            return carry

        lax.fori_loop(0, per_piece, group_step, 0)
        span = pl.ds(j * per_piece, per_piece)
        for k in range(own):
            pltpu.make_async_remote_copy(
                src_ref=ob.at[k, span], dst_ref=ib.at[back[k], span],
                send_sem=os_sem.at[0], recv_sem=or_sem.at[0],
                device_id=(p, mate(k)), device_id_type=MESH,
            ).start()
        return carry

    lax.fori_loop(0, pieces, piece_step, 0)
    for k in range(own):
        pltpu.make_async_remote_copy(
            src_ref=ob.at[k, half], dst_ref=ib.at[back[k], half],
            send_sem=os_sem.at[0], recv_sem=or_sem.at[0],
            device_id=(p, mate(k)), device_id_type=MESH,
        ).start()
    ib[own] = ob[own]
    drain(ib.at[pl.ds(0, own)], or_sem.at[0])

    small = lax.broadcasted_iota(jnp.int32, (HG, DH), 1)
    for side in range(2):
        core = (c + side) % 2
        sources = [k for k in range(nreq) if offsets[k][2] == side]
        stat = [ib[k, half].astype(F32) for k in sources]
        top = functools.reduce(jnp.maximum, stat)
        factor = [jnp.exp2(t - top) for t in stat]
        total = functools.reduce(
            jnp.add,
            [t * pltpu.roll(f, 1, 1) for t, f in zip(stat, factor)],
        )
        rest = functools.reduce(jnp.add, [t * pltpu.roll(f, 2, 1) for t, f in zip(stat, factor)])
        for i in range(half):
            g = half * core + i
            num = functools.reduce(
                jnp.add,
                [f[:, 4 * i : 4 * i + 1] * ib[k, i].astype(F32) for k, f in zip(sources, factor)],
            )
            peak = top[:, 4 * i : 4 * i + 1]
            l = total[:, 4 * i + 1 : 4 * i + 2] + rest[:, 4 * i + 2 : 4 * i + 3]
            sm = sml[g, 0]
            both = jnp.maximum(sm, peak)
            fp = jnp.exp2(peak - both)
            fs = jnp.exp2(sm - both)
            num = num * fp + sn[g] * fs
            l = l * fp + sml[g, 1] * fs
            high = l.astype(BF16).astype(F32)
            zo[g, 0] = num.astype(BF16)
            zo[g, 1] = jnp.where(small == 0, both, jnp.where(small == 1, high, l - high)).astype(BF16)

    for k in far_first:
        target = pre_mate(k)
        pltpu.make_async_remote_copy(
            src_ref=zo.at[target], dst_ref=zi.at[p], send_sem=zz_sem.at[0], recv_sem=zz_sem.at[1],
            device_id=(target, r), device_id_type=MESH,
        ).start()
    zi[p] = zo[p]
    drain(zi.at[pl.ds(0, npre - 1)], zz_sem.at[1])
    stat = [zi[i, 1].astype(F32) for i in range(npre)]
    peaks = [t[:, 0:1] for t in stat]
    top = functools.reduce(jnp.maximum, peaks)
    factor = [jnp.exp2(t - top) for t in peaks]
    num = functools.reduce(jnp.add, [f * zi[i, 0].astype(F32) for i, f in enumerate(factor)])
    l = functools.reduce(jnp.add, [f * (t[:, 1:2] + t[:, 2:3]) for f, t in zip(factor, stat)])
    result = (num / l).astype(BF16)
    for h in range(HG):
        out_ref[:, h * DH : (h + 1) * DH] = result[h : h + 1]

    drain(qz.at[pl.ds(0, npre - 1)], z_sem.at[0])
    drain(keys, kv_sem.at[0])
    drain(values, kv_sem.at[1])
    drain(qa.at[pl.ds(0, own)], qs_sem.at[0])
    drain(ib.at[pl.ds(0, own)], os_sem.at[0])
    drain(zi.at[pl.ds(0, npre - 1)], zz_sem.at[0])


def on_device(dims, pieces, row_chunks, queries, prefix_keys, prefix_values, suffix_keys, suffix_values, suffix_lengths):
    npre, nx, ny = dims
    nreq = nx * ny * 2
    half = npre // 2
    tokens = prefix_keys.shape[0]
    slots = suffix_keys.shape[1]
    width = npre * DH
    vmem = pl.BlockSpec(memory_space=pltpu.VMEM)
    hbm = pl.BlockSpec(memory_space=pl.ANY)
    dma = pltpu.SemaphoreType.DMA
    return pl.pallas_call(
        functools.partial(kernel, dims, pieces, row_chunks),
        out_shape=jax.ShapeDtypeStruct((1, HG * DH), BF16),
        in_specs=[vmem, hbm, hbm, hbm, hbm, pl.BlockSpec(memory_space=pltpu.SMEM)],
        out_specs=vmem,
        scratch_shapes=[
            pltpu.VMEM((half, 2 * tokens, DH), BF16),
            pltpu.VMEM((half, 2 * tokens, 2 * DH), BF16),
            pltpu.VMEM((slots, width), BF16),
            pltpu.VMEM((slots, width), BF16),
            pltpu.VMEM((npre, HG, DH), BF16),
            pltpu.VMEM((nreq, half, HG, DH), BF16),
            pltpu.VMEM((nreq, half + 1, HG, DH), BF16),
            pltpu.VMEM((nreq, half + 1, HG, DH), BF16),
            pltpu.VMEM((npre, 2, HG, DH), BF16),
            pltpu.VMEM((npre, 2, HG, DH), BF16),
            pltpu.VMEM((npre, HG, DH), F32),
            pltpu.VMEM((npre, 2, HG, DH), F32),
            dma((4,)),
            dma((4,)),
            dma((2,)),
            dma((1,)),
            dma((pieces,)),
            dma((1,)),
            dma((1,)),
            dma((2,)),
        ],
        compiler_params=pltpu.CompilerParams(
            collective_id=0, has_side_effects=True, vmem_limit_bytes=60 * 1024 * 1024
        ),
    )(queries, prefix_keys, prefix_values, suffix_keys, suffix_values, suffix_lengths)


def build(mesh, dims, pieces, row_chunks):
    placed = (
        P("req", "pre"),
        P(("pre", "req"), None),
        P(("pre", "req"), None),
        P("req", "pre", None),
        P("req", "pre", None),
        P("req"),
    )
    return jax.shard_map(
        functools.partial(on_device, dims, pieces, row_chunks),
        mesh=mesh, in_specs=placed, out_specs=P("req", "pre"), check_vma=False,
    )


def solution(mesh):
    return build(mesh, (8, 4, 4), 4, 4)
```

```python
import functools
import math

import jax
import jax.numpy as jnp
from jax import lax
from jax.experimental import pallas as pl
from jax.experimental.pallas import tpu as pltpu
from jax.sharding import PartitionSpec as P

MESH = pl.DeviceIdType.MESH
DH = 128
HG = 16
F32 = jnp.float32
BF16 = jnp.bfloat16
SCALE = math.log2(math.e) / math.sqrt(DH)
NEG = -1e30


def ring(n):
    order = [0]
    for d in range(1, n // 2 + 1):
        order += [d] if 2 * d == n else [d, n - d]
    counts = [sum(min(o, n - o) == d for o in order) for d in range(n // 2 + 1)]
    return order, counts


def plane_chips(nx, ny):
    def hops(o):
        return min(o[0], nx - o[0]) + min(o[1], ny - o[1])

    chips = sorted([(i, j) for i in range(nx) for j in range(ny)], key=lambda o: -hops(o))
    back = [chips.index(((-i) % nx, (-j) % ny)) for i, j in chips]
    return chips, back


def kernel(
    dims, row_chunks,
    q_ref, k_ref, v_ref, sk_ref, sv_ref, len_ref, out_ref,
    qrow, length, kb, vx, skb, svb, qz, qa, ob, ib, acc, st, ist, zo, zi, zst, zist, sn, sml,
    local_sem, kvs_sem, kvr_sem, zs_sem, zr_sem, qs_sem, qr_sem, os_sem, or_sem, zz_sem,
):
    npre, nx, ny = dims
    nreq = nx * ny * 2
    half = npre // 2
    tokens = k_ref.shape[0]
    slots = sk_ref.shape[1]
    p = lax.axis_index("pre")
    r = lax.axis_index("req")
    c = r % 2
    e = (p + c) % 2
    x = r // (2 * ny)
    y = (r // 2) % ny
    order, counts = ring(npre)
    first = [sum(counts[:d]) for d in range(len(counts))]
    work = [[o for o in order if o % 2 == s] for s in range(2)]
    chips, back = plane_chips(nx, ny)
    others = nreq - 1
    own_chip = len(chips) - 1

    def plane_mate(chip, core):
        kx, ky = chips[chip]
        return (((x + kx) % nx) * ny + (y + ky) % ny) * 2 + (c + core) % 2

    def pre_mate(k):
        return (p + k) % npre

    def offset(parity, i):
        return work[0][i] + parity * (work[1][i] - work[0][i])

    def columns(parity, i):
        return pl.ds(pl.multiple_of(((p + offset(parity, i)) % npre) * DH, DH), DH)

    def own_rows():
        return pl.ds(pl.multiple_of(c * tokens, tokens), tokens)

    def drain(ref, sem):
        pltpu.make_async_copy(ref, ref, sem).wait()

    plane = [(n, core) for n in range(len(chips)) for core in range(2)]
    barrier = pltpu.get_barrier_semaphore()
    for n, core in plane:
        if (n, core) != (own_chip, 0):
            pl.semaphore_signal(barrier, inc=1, device_id=(p, plane_mate(n, core)), device_id_type=MESH)
    for k in range(1, npre):
        pl.semaphore_signal(barrier, inc=1, device_id=(pre_mate(k), r), device_id_type=MESH)

    query_copy = pltpu.make_async_copy(q_ref, qrow, local_sem.at[4])
    query_copy.start()
    length_copy = pltpu.make_async_copy(len_ref, length, local_sem.at[5])
    length_copy.start()
    for i in range(half):
        pltpu.make_async_copy(k_ref.at[:, columns(e, i)], kb.at[i, own_rows(), :], local_sem.at[0]).start()
        pltpu.make_async_copy(
            v_ref.at[:, columns(e, i)], vx.at[i, own_rows(), pl.ds(0, DH)], local_sem.at[1]
        ).start()
    suffix = [
        pltpu.make_async_copy(sk_ref.at[0], skb, local_sem.at[2]),
        pltpu.make_async_copy(sv_ref.at[0], svb, local_sem.at[3]),
    ]
    for copy in suffix:
        copy.start()

    query_copy.wait()
    tile = jnp.concatenate([qrow[:, h * DH : (h + 1) * DH].astype(F32) for h in range(HG)], axis=0)
    qz[0] = tile.astype(BF16)
    acc[...] = jnp.zeros_like(acc)

    def fill(i, carry):
        vx[i, :, DH : 2 * DH] = jnp.ones((2 * tokens, DH), BF16)
        return carry

    lax.fori_loop(0, half, fill, 0)
    pl.semaphore_wait(barrier, npre - 1 + others)

    for k in reversed(order[1:]):
        distance = min(k, npre - k)
        pltpu.make_async_remote_copy(
            src_ref=qz.at[0], dst_ref=qz.at[order.index(npre - k)],
            send_sem=zs_sem.at[0], recv_sem=zr_sem.at[distance],
            device_id=(pre_mate(k), r), device_id_type=MESH,
        ).start()

    starts = {}
    for d, count in enumerate(counts):
        starts[d] = sum(counts[d % 2 : d : 2])

    def forward(d):
        count = counts[d]
        core = (d + e) % 2
        src = qz.at[pl.ds(first[d], count)]
        for n in range(own_chip):
            pltpu.make_async_remote_copy(
                src_ref=src, dst_ref=qa.at[2 * back[n] + core, pl.ds(starts[d], count)],
                send_sem=qs_sem.at[d], recv_sem=qr_sem.at[d],
                device_id=(p, plane_mate(n, core)), device_id_type=MESH,
            ).start()

        @pl.when(core == 1)
        def _():
            pltpu.make_async_remote_copy(
                src_ref=src, dst_ref=qa.at[2 * own_chip + 1, pl.ds(starts[d], count)],
                send_sem=qs_sem.at[d], recv_sem=qr_sem.at[d],
                device_id=(p, plane_mate(own_chip, 1)), device_id_type=MESH,
            ).start()

        @pl.when(core == 0)
        def _():
            qa[2 * own_chip, starts[d] : starts[d] + count] = qz[first[d] : first[d] + count]

    forward(0)

    sib = plane_mate(own_chip, 1)
    for i in range(half):
        for n, (src, dst) in enumerate(
            (
                (k_ref.at[:, columns(1 - e, i)], kb.at[i, own_rows(), :]),
                (v_ref.at[:, columns(1 - e, i)], vx.at[i, own_rows(), pl.ds(0, DH)]),
            )
        ):
            pltpu.make_async_remote_copy(
                src_ref=src, dst_ref=dst, send_sem=kvs_sem.at[n], recv_sem=kvr_sem.at[n, i],
                device_id=(p, sib), device_id_type=MESH,
            ).start()

    for d in range(1, len(counts)):
        drain(qz.at[pl.ds(0, counts[d])], zr_sem.at[d])
        forward(d)

    keys, values = kb.at[:, pl.ds(0, tokens), :], vx.at[:, pl.ds(0, tokens), pl.ds(0, DH)]
    drain(keys, local_sem.at[0])
    drain(values, local_sem.at[1])

    chunk = nreq // row_chunks
    lane = lax.broadcasted_iota(jnp.int32, (chunk * HG, DH), 1)
    head = lax.broadcasted_iota(jnp.int32, (chunk * HG, DH), 0) % HG

    def group_step(i, carry):
        drain(kb.at[0, pl.ds(0, tokens)], kvr_sem.at[0, i])
        drain(vx.at[0, pl.ds(0, tokens), pl.ds(0, DH)], kvr_sem.at[1, i])
        for d, count in enumerate(counts):

            @pl.when((e == d % 2) & (i == starts[d]))
            def _(d=d, count=count):
                drain(qa.at[pl.ds(0, others), pl.ds(0, count)], qr_sem.at[d])

        for ch in range(row_chunks):
            rows = pl.ds(ch * chunk, chunk)
            qc = qa[rows, i].reshape(chunk * HG, DH)
            s = lax.dot_general(qc, kb[i], (((1,), (1,)), ((), ())), preferred_element_type=F32)
            m = (jnp.max(s, axis=1, keepdims=True) * SCALE).astype(BF16).astype(F32)
            w = jnp.exp2(s * SCALE - m).astype(BF16)
            o = jnp.dot(w, vx[i], preferred_element_type=F32)
            ob[rows, i] = o[:, :DH].astype(BF16).reshape(chunk, HG, DH)
            stats = jnp.where(lane == HG * i + head, m, 0.0)
            stats = jnp.where(lane == DH // 2 + HG * i + head, o[:, DH:], stats)
            acc[rows] += jnp.sum(stats.reshape(chunk, HG, DH), axis=1)
        for n, core in plane:
            if (n, core) != (own_chip, 0):
                pltpu.make_async_remote_copy(
                    src_ref=ob.at[2 * n + core, i], dst_ref=ib.at[2 * back[n] + core, i],
                    send_sem=os_sem.at[0], recv_sem=or_sem.at[0],
                    device_id=(p, plane_mate(n, core)), device_id_type=MESH,
                ).start()
        return carry

    lax.fori_loop(0, half, group_step, 0)
    for k in range(nreq):
        st[k] = acc[k : k + 1]
    for n, core in plane:
        if (n, core) != (own_chip, 0):
            pltpu.make_async_remote_copy(
                src_ref=st.at[2 * n + core], dst_ref=ist.at[2 * back[n] + core],
                send_sem=os_sem.at[1], recv_sem=or_sem.at[1],
                device_id=(p, plane_mate(n, core)), device_id_type=MESH,
            ).start()
    ib[2 * own_chip] = ob[2 * own_chip]
    ist[2 * own_chip] = st[2 * own_chip]

    length_copy.wait()
    for copy in suffix:
        copy.wait()
    visible = (p * slots + lax.broadcasted_iota(jnp.int32, (HG, slots), 1)) < length[0]
    for t, k in enumerate(order):
        span = pl.ds(pl.multiple_of(pre_mate(k) * DH, DH), DH)
        s = lax.dot_general(qz[t], skb[:, span], (((1,), (1,)), ((), ())), preferred_element_type=F32)
        s = jnp.where(visible, s * SCALE, NEG)
        m = jnp.max(s, axis=1, keepdims=True)
        w = jnp.where(visible, jnp.exp2(s - m), 0.0).astype(BF16)
        sn[k] = jnp.dot(w, svb[:, span], preferred_element_type=F32)
        l = jnp.sum(w.astype(F32), axis=1, keepdims=True)
        sml[k, 0] = jnp.broadcast_to(m, (HG, DH))
        sml[k, 1] = jnp.broadcast_to(l, (HG, DH))

    drain(ib.at[pl.ds(0, others)], or_sem.at[0])
    drain(ist.at[pl.ds(0, others)], or_sem.at[1])

    lane = lax.broadcasted_iota(jnp.int32, (HG, DH), 1)
    head = lax.broadcasted_iota(jnp.int32, (HG, DH), 0)

    def weigh(rows, shift):
        table = jnp.concatenate(rows, axis=0)
        top = jnp.max(table, axis=0, keepdims=True)
        factor = jnp.exp2(table - top)
        total = jnp.sum(factor * pltpu.roll(table, DH - shift, 1), axis=0, keepdims=True)
        pad = jnp.zeros(((-len(rows) - 2) % 8, DH), F32)
        return jnp.concatenate([factor, top, total, pad], axis=0).T

    for side in range(2):
        parity = (e + side) % 2
        sources = [2 * n + side for n in range(len(chips))]
        columns_of = weigh([ist[k] for k in sources], DH // 2)
        for i in range(half):
            part = columns_of[HG * i : HG * (i + 1)]
            num = functools.reduce(
                jnp.add, [part[:, n : n + 1] * ib[k, i].astype(F32) for n, k in enumerate(sources)]
            )
            peak = part[:, len(chips) : len(chips) + 1]
            l = part[:, len(chips) + 1 : len(chips) + 2]
            k = offset(parity, i)
            sm = sml[k, 0]
            both = jnp.maximum(sm, peak)
            fp = jnp.exp2(peak - both)
            fs = jnp.exp2(sm - both)
            num = num * fp + sn[k] * fs
            l = l * fp + sml[k, 1] * fs
            zo[k] = num.astype(BF16)
            stats = jnp.where(lane == head, both, jnp.where(lane == HG + head, l, 0.0))
            zst[k] = jnp.sum(stats, axis=0, keepdims=True)

    for k in reversed(order[1:]):
        for n, (src, dst) in enumerate(((zo, zi), (zst, zist))):
            pltpu.make_async_remote_copy(
                src_ref=src.at[k], dst_ref=dst.at[npre - k], send_sem=zz_sem.at[n], recv_sem=zz_sem.at[2 + n],
                device_id=(pre_mate(k), r), device_id_type=MESH,
            ).start()
    zi[0] = zo[0]
    zist[0] = zst[0]
    drain(zist.at[pl.ds(0, npre - 1)], zz_sem.at[3])
    columns_of = weigh([zist[k] for k in range(npre)], HG)[:HG]
    drain(zi.at[pl.ds(0, npre - 1)], zz_sem.at[2])
    num = functools.reduce(jnp.add, [columns_of[:, k : k + 1] * zi[k].astype(F32) for k in range(npre)])
    result = (num / columns_of[:, npre + 1 : npre + 2]).astype(BF16)
    for h in range(HG):
        out_ref[:, h * DH : (h + 1) * DH] = result[h : h + 1]

    drain(qz.at[pl.ds(0, npre - 1)], zs_sem.at[0])
    drain(keys, kvs_sem.at[0])
    drain(values, kvs_sem.at[1])
    for d, count in enumerate(counts):
        core = (d + e) % 2

        @pl.when(core == 1)
        def _(d=d, count=count):
            drain(qa.at[pl.ds(0, len(chips)), pl.ds(0, count)], qs_sem.at[d])

        @pl.when(core == 0)
        def _(d=d, count=count):
            drain(qa.at[pl.ds(0, own_chip), pl.ds(0, count)], qs_sem.at[d])

    drain(ib.at[pl.ds(0, others)], os_sem.at[0])
    drain(ist.at[pl.ds(0, others)], os_sem.at[1])
    drain(zi.at[pl.ds(0, npre - 1)], zz_sem.at[0])
    drain(zist.at[pl.ds(0, npre - 1)], zz_sem.at[1])


def on_device(dims, row_chunks, queries, prefix_keys, prefix_values, suffix_keys, suffix_values, suffix_lengths):
    npre, nx, ny = dims
    nreq = nx * ny * 2
    half = npre // 2
    tokens = prefix_keys.shape[0]
    slots = suffix_keys.shape[1]
    width = npre * DH
    vmem = pl.BlockSpec(memory_space=pltpu.VMEM)
    hbm = pl.BlockSpec(memory_space=pl.ANY)
    dma = pltpu.SemaphoreType.DMA
    distances = half + 1
    return pl.pallas_call(
        functools.partial(kernel, dims, row_chunks),
        out_shape=pltpu.VMEM((1, HG * DH), BF16),
        in_specs=[hbm] * 6,
        out_specs=vmem,
        scratch_shapes=[
            pltpu.VMEM((1, HG * DH), BF16),
            pltpu.SMEM((1,), jnp.int32),
            pltpu.VMEM((half, 2 * tokens, DH), BF16),
            pltpu.VMEM((half, 2 * tokens, 2 * DH), BF16),
            pltpu.VMEM((slots, width), BF16),
            pltpu.VMEM((slots, width), BF16),
            pltpu.VMEM((npre, HG, DH), BF16),
            pltpu.VMEM((nreq, half, HG, DH), BF16),
            pltpu.VMEM((nreq, half, HG, DH), BF16),
            pltpu.VMEM((nreq, half, HG, DH), BF16),
            pltpu.VMEM((nreq, DH), F32),
            pltpu.VMEM((nreq, 1, DH), F32),
            pltpu.VMEM((nreq, 1, DH), F32),
            pltpu.VMEM((npre, HG, DH), BF16),
            pltpu.VMEM((npre, HG, DH), BF16),
            pltpu.VMEM((npre, 1, DH), F32),
            pltpu.VMEM((npre, 1, DH), F32),
            pltpu.VMEM((npre, HG, DH), F32),
            pltpu.VMEM((npre, 2, HG, DH), F32),
            dma((6,)),
            dma((2,)),
            dma((2, half)),
            dma((1,)),
            dma((distances,)),
            dma((distances,)),
            dma((distances,)),
            dma((2,)),
            dma((2,)),
            dma((4,)),
        ],
        compiler_params=pltpu.CompilerParams(
            collective_id=0, has_side_effects=True, vmem_limit_bytes=60 * 1024 * 1024
        ),
    )(queries, prefix_keys, prefix_values, suffix_keys, suffix_values, suffix_lengths)


def build(mesh, dims, row_chunks):
    placed = (
        P("req", "pre"),
        P(("pre", "req"), None),
        P(("pre", "req"), None),
        P("req", "pre", None),
        P("req", "pre", None),
        P("req"),
    )
    return jax.shard_map(
        functools.partial(on_device, dims, row_chunks),
        mesh=mesh, in_specs=placed, out_specs=P("req", "pre"), check_vma=False,
    )


def solution(mesh):
    return build(mesh, (8, 4, 4), 4)
```

```python
import functools
import math

import jax
import jax.numpy as jnp
from jax import lax
from jax.experimental import pallas as pl
from jax.experimental.pallas import tpu as pltpu
from jax.sharding import PartitionSpec as P

MESH = pl.DeviceIdType.MESH
DH = 128
HG = 16
F32 = jnp.float32
BF16 = jnp.bfloat16
SCALE = math.log2(math.e) / math.sqrt(DH)
NEG = -1e30


def plane_chips(nx, ny):
    def hops(o):
        return min(o[0], nx - o[0]) + min(o[1], ny - o[1])

    chips = sorted([(i, j) for i in range(nx) for j in range(ny)], key=lambda o: -hops(o))
    back = [chips.index(((-i) % nx, (-j) % ny)) for i, j in chips]
    return chips, back


def kernel(
    dims, row_chunks,
    q_ref, k_ref, v_ref, sk_ref, sv_ref, len_ref, out_ref,
    qrow, length, kb, vx, skb, svb, qz, qa, ob, ib, st, ist, zo, zi, zst, zist, so, sst,
    local_sem, kvs_sem, kvr_sem, zs_sem, zr_sem, qs_sem, qr_sem, os_sem, or_sem, zz_sem, su_sem,
):
    npre, nx, ny = dims
    nreq = nx * ny * 2
    half = npre // 2
    tokens = k_ref.shape[0]
    slots = sk_ref.shape[1]
    p = lax.axis_index("pre")
    r = lax.axis_index("req")
    c = r % 2
    e = (p + c) % 2
    x = r // (2 * ny)
    y = (r // 2) % ny
    chips, back = plane_chips(nx, ny)
    others = nreq - 1
    own_chip = len(chips) - 1

    def plane_mate(chip, core):
        kx, ky = chips[chip]
        return (((x + kx) % nx) * ny + (y + ky) % ny) * 2 + (c + core) % 2

    def pre_mate(k):
        return (p + k) % npre

    def columns(g):
        return pl.ds(pl.multiple_of(g * DH, DH), DH)

    def own_rows():
        return pl.ds(pl.multiple_of(c * tokens, tokens), tokens)

    def drain(ref, sem):
        pltpu.make_async_copy(ref, ref, sem).wait()

    plane = [(n, core) for n in range(len(chips)) for core in range(2)]
    barrier = pltpu.get_barrier_semaphore()
    for n, core in plane:
        if (n, core) != (own_chip, 0):
            pl.semaphore_signal(barrier, inc=1, device_id=(p, plane_mate(n, core)), device_id_type=MESH)
    sib = plane_mate(own_chip, 1)
    for k in range(1, npre):
        for mate in (r, sib):
            pl.semaphore_signal(barrier, inc=1, device_id=(pre_mate(k), mate), device_id_type=MESH)

    query_copy = pltpu.make_async_copy(q_ref, qrow, local_sem.at[4])
    query_copy.start()
    length_copy = pltpu.make_async_copy(len_ref, length, local_sem.at[5])
    length_copy.start()
    for i in range(half):
        pltpu.make_async_copy(k_ref.at[:, columns(2 * i + c)], kb.at[i, own_rows(), :], local_sem.at[0]).start()
        pltpu.make_async_copy(
            v_ref.at[:, columns(2 * i + c)], vx.at[i, own_rows(), pl.ds(0, DH)], local_sem.at[1]
        ).start()
    suffix = [
        pltpu.make_async_copy(sk_ref.at[0], skb, local_sem.at[2]),
        pltpu.make_async_copy(sv_ref.at[0], svb, local_sem.at[3]),
    ]
    for copy in suffix:
        copy.start()

    query_copy.wait()
    tile = jnp.concatenate([qrow[:, h * DH : (h + 1) * DH].astype(F32) for h in range(HG)], axis=0)
    qz[p] = tile.astype(BF16)

    def fill(i, carry):
        vx[i, :, DH : 2 * DH] = jnp.ones((2 * tokens, DH), BF16)
        return carry

    lax.fori_loop(0, half, fill, 0)
    pl.semaphore_wait(barrier, 2 * (npre - 1) + others)

    far_first = sorted(range(1, npre), key=lambda k: -min(k, npre - k))
    for k in far_first:
        pltpu.make_async_remote_copy(
            src_ref=qz.at[p], dst_ref=qz.at[p], send_sem=zs_sem.at[0], recv_sem=zr_sem.at[p],
            device_id=(pre_mate(k), r), device_id_type=MESH,
        ).start()

    def forward(g):
        @pl.when(p != g)
        def _():
            drain(qz.at[g], zr_sem.at[g])

        core = (g + c) % 2
        for n in range(own_chip):
            pltpu.make_async_remote_copy(
                src_ref=qz.at[g], dst_ref=qa.at[2 * back[n] + core, g // 2],
                send_sem=qs_sem.at[g], recv_sem=qr_sem.at[g],
                device_id=(p, plane_mate(n, core)), device_id_type=MESH,
            ).start()

        @pl.when(core == 1)
        def _():
            pltpu.make_async_remote_copy(
                src_ref=qz.at[g], dst_ref=qa.at[2 * own_chip + 1, g // 2],
                send_sem=qs_sem.at[g], recv_sem=qr_sem.at[g],
                device_id=(p, sib), device_id_type=MESH,
            ).start()

        @pl.when(core == 0)
        def _():
            qa[2 * own_chip, g // 2] = qz[g]

    for i in range(half):
        for n, (src, dst) in enumerate(
            (
                (k_ref.at[:, columns(2 * i + 1 - c)], kb.at[i, own_rows(), :]),
                (v_ref.at[:, columns(2 * i + 1 - c)], vx.at[i, own_rows(), pl.ds(0, DH)]),
            )
        ):
            pltpu.make_async_remote_copy(
                src_ref=src, dst_ref=dst, send_sem=kvs_sem.at[n], recv_sem=kvr_sem.at[n, i],
                device_id=(p, sib), device_id_type=MESH,
            ).start()

    def as_row(peak, total, lanes):
        count = peak.shape[0]
        at = lax.broadcasted_iota(jnp.int32, (count, DH), 1)
        row = lax.broadcasted_iota(jnp.int32, (count, DH), 0)
        return jnp.sum(jnp.where(at == row, peak, jnp.where(at == lanes + row, total, 0.0)), axis=0, keepdims=True)

    def weigh(rows, lanes):
        table = jnp.concatenate(rows, axis=0)
        top = jnp.max(table, axis=0, keepdims=True)
        factor = jnp.exp2(table - top)
        total = jnp.sum(factor * pltpu.roll(table, DH - lanes, 1), axis=0, keepdims=True)
        pad = jnp.zeros(((-len(rows) - 2) % 8, DH), F32)
        return jnp.concatenate([factor, top, total, pad], axis=0).T

    length_copy.wait()
    for copy in suffix:
        copy.wait()
    visible = (p * slots + lax.broadcasted_iota(jnp.int32, (HG, slots), 1)) < length[0]

    def suffix_part(g):
        span = slice(g * DH, (g + 1) * DH)
        s = lax.dot_general(qz[g], skb[:, span], (((1,), (1,)), ((), ())), preferred_element_type=F32)
        s = jnp.where(visible, s * SCALE, NEG)
        m = jnp.max(s, axis=1, keepdims=True)
        w = jnp.where(visible, jnp.exp2(s - m), 0.0).astype(BF16)
        so[g] = jnp.dot(w, svb[:, span], preferred_element_type=F32).astype(BF16)
        sst[g] = as_row(m, jnp.sum(w.astype(F32), axis=1, keepdims=True), HG)

    for low, high in ((0, half), (half, npre)):
        for g in range(low, high):
            forward(g)
        for g in range(low, high):
            suffix_part(g)
    for k in far_first:
        g = pre_mate(k)
        for n, (src, dst) in enumerate(((so, zi), (sst, zist))):
            pltpu.make_async_remote_copy(
                src_ref=src.at[g], dst_ref=dst.at[npre + p], send_sem=su_sem.at[n], recv_sem=su_sem.at[2 + n],
                device_id=(g, r), device_id_type=MESH,
            ).start()
    zi[npre + p] = so[p]
    zist[npre + p] = sst[p]

    keys, values = kb.at[:, pl.ds(0, tokens), :], vx.at[:, pl.ds(0, tokens), pl.ds(0, DH)]
    drain(keys, local_sem.at[0])
    drain(values, local_sem.at[1])

    chunk = nreq // row_chunks
    per = chunk // 2
    pair_lane = lax.broadcasted_iota(jnp.int32, (chunk * HG, DH), 1)
    pair_row = lax.broadcasted_iota(jnp.int32, (chunk * HG, DH), 0) % (2 * HG)

    def group_step(i, carry):
        drain(kb.at[0, pl.ds(0, tokens)], kvr_sem.at[0, i])
        drain(vx.at[0, pl.ds(0, tokens), pl.ds(0, DH)], kvr_sem.at[1, i])
        drain(qa.at[pl.ds(0, others), 0], qr_sem.at[2 * i + c])

        def scores(ch):
            qc = qa[pl.ds(ch * chunk, chunk), i].reshape(chunk * HG, DH)
            return lax.dot_general(qc, kb[i], (((1,), (1,)), ((), ())), preferred_element_type=F32)

        s = scores(0)
        for ch in range(row_chunks):
            after = scores(ch + 1) if ch + 1 < row_chunks else None
            m = (jnp.max(s, axis=1, keepdims=True) * SCALE).astype(BF16).astype(F32)
            w = jnp.exp2(s * SCALE - m).astype(BF16)
            o = jnp.dot(w, vx[i], preferred_element_type=F32)
            ob[i, pl.ds(ch * per, per)] = o[:, :DH].astype(BF16).reshape(per, 2, HG, DH)
            stats = jnp.where(pair_lane == pair_row, m, 0.0)
            stats = jnp.where(pair_lane == DH // 2 + pair_row, o[:, DH:], stats)
            rows = jnp.sum(stats.reshape(per, 2 * HG, DH), axis=1)
            for n in range(per):
                st[i, ch * per + n] = rows[n : n + 1]
            s = after
        for n in range(own_chip):
            for a, (src, dst) in enumerate(((ob, ib), (st, ist))):
                pltpu.make_async_remote_copy(
                    src_ref=src.at[i, n], dst_ref=dst.at[i, back[n]],
                    send_sem=os_sem.at[a], recv_sem=or_sem.at[a, i],
                    device_id=(p, plane_mate(n, 0)), device_id_type=MESH,
                ).start()
        ib[i, own_chip] = ob[i, own_chip]
        ist[i, own_chip] = st[i, own_chip]
        return carry

    lax.fori_loop(0, half, group_step, 0)

    def combine_step(i, carry):
        drain(ist.at[i, pl.ds(0, own_chip)], or_sem.at[1, i])
        columns_of = weigh([ist[i, n] for n in range(len(chips))], DH // 2)[: 2 * HG]
        drain(ib.at[i, pl.ds(0, own_chip)], or_sem.at[0, i])
        num = functools.reduce(
            jnp.add,
            [columns_of[:, n : n + 1] * ib[i, n].reshape(2 * HG, DH).astype(F32) for n in range(len(chips))],
        )
        zo[i] = num.astype(BF16).reshape(2, HG, DH)
        for core in range(2):
            part = columns_of[HG * core : HG * (core + 1)]
            zst[i, core] = as_row(part[:, len(chips) : len(chips) + 1], part[:, len(chips) + 1 : len(chips) + 2], HG)
        g = 2 * i + c

        def send(core):
            for n, (src, dst) in enumerate(((zo, zi), (zst, zist))):
                pltpu.make_async_remote_copy(
                    src_ref=src.at[i, core], dst_ref=dst.at[p], send_sem=zz_sem.at[n], recv_sem=zz_sem.at[2 + n],
                    device_id=(g, sib if core else r), device_id_type=MESH,
                ).start()

        send(1)

        @pl.when(g != p)
        def _():
            send(0)

        @pl.when(g == p)
        def _():
            zi[p] = zo[i, 0]
            zist[p] = zst[i, 0]

        return carry

    lax.fori_loop(0, half, combine_step, 0)

    def both_cores(array, sem):
        @pl.when(e == 0)
        def _():
            drain(array.at[pl.ds(0, npre - 1)], sem)

        @pl.when(e == 1)
        def _():
            drain(array.at[pl.ds(0, npre)], sem)

    drain(zi.at[pl.ds(0, npre - 1)], su_sem.at[2])
    drain(zist.at[pl.ds(0, npre - 1)], su_sem.at[3])
    both_cores(zist, zz_sem.at[3])
    columns_of = weigh([zist[k] for k in range(2 * npre)], HG)[:HG]
    both_cores(zi, zz_sem.at[2])
    num = functools.reduce(jnp.add, [columns_of[:, k : k + 1] * zi[k].astype(F32) for k in range(2 * npre)])
    result = (num / columns_of[:, 2 * npre + 1 : 2 * npre + 2]).astype(BF16)
    for h in range(HG):
        out_ref[:, h * DH : (h + 1) * DH] = result[h : h + 1]

    drain(qz.at[pl.ds(0, npre - 1)], zs_sem.at[0])
    drain(keys, kvs_sem.at[0])
    drain(values, kvs_sem.at[1])
    for g in range(npre):
        core = (g + c) % 2

        @pl.when(core == 1)
        def _(g=g):
            drain(qa.at[pl.ds(0, len(chips)), 0], qs_sem.at[g])

        @pl.when(core == 0)
        def _(g=g):
            drain(qa.at[pl.ds(0, own_chip), 0], qs_sem.at[g])

    drain(ib.at[:, pl.ds(0, own_chip)], os_sem.at[0])
    drain(ist.at[:, pl.ds(0, own_chip)], os_sem.at[1])
    drain(zi.at[pl.ds(0, npre - 1)], su_sem.at[0])
    drain(zist.at[pl.ds(0, npre - 1)], su_sem.at[1])
    both_cores(zi, zz_sem.at[0])
    both_cores(zist, zz_sem.at[1])


def on_device(dims, row_chunks, queries, prefix_keys, prefix_values, suffix_keys, suffix_values, suffix_lengths):
    npre, nx, ny = dims
    nreq = nx * ny * 2
    half = npre // 2
    tokens = prefix_keys.shape[0]
    slots = suffix_keys.shape[1]
    width = npre * DH
    vmem = pl.BlockSpec(memory_space=pltpu.VMEM)
    hbm = pl.BlockSpec(memory_space=pl.ANY)
    dma = pltpu.SemaphoreType.DMA
    return pl.pallas_call(
        functools.partial(kernel, dims, row_chunks),
        out_shape=pltpu.VMEM((1, HG * DH), BF16),
        in_specs=[hbm] * 6,
        out_specs=vmem,
        scratch_shapes=[
            pltpu.VMEM((1, HG * DH), BF16),
            pltpu.SMEM((1,), jnp.int32),
            pltpu.VMEM((half, 2 * tokens, DH), BF16),
            pltpu.VMEM((half, 2 * tokens, 2 * DH), BF16),
            pltpu.VMEM((slots, width), BF16),
            pltpu.VMEM((slots, width), BF16),
            pltpu.VMEM((npre, HG, DH), BF16),
            pltpu.VMEM((nreq, half, HG, DH), BF16),
            pltpu.VMEM((half, nreq // 2, 2, HG, DH), BF16),
            pltpu.VMEM((half, nreq // 2, 2, HG, DH), BF16),
            pltpu.VMEM((half, nreq // 2, 1, DH), F32),
            pltpu.VMEM((half, nreq // 2, 1, DH), F32),
            pltpu.VMEM((half, 2, HG, DH), BF16),
            pltpu.VMEM((2 * npre, HG, DH), BF16),
            pltpu.VMEM((half, 2, 1, DH), F32),
            pltpu.VMEM((2 * npre, 1, DH), F32),
            pltpu.VMEM((npre, HG, DH), BF16),
            pltpu.VMEM((npre, 1, DH), F32),
            dma((6,)),
            dma((2,)),
            dma((2, half)),
            dma((1,)),
            dma((npre,)),
            dma((npre,)),
            dma((npre,)),
            dma((2,)),
            dma((2, half)),
            dma((4,)),
            dma((4,)),
        ],
        compiler_params=pltpu.CompilerParams(
            collective_id=0, has_side_effects=True, vmem_limit_bytes=60 * 1024 * 1024
        ),
    )(queries, prefix_keys, prefix_values, suffix_keys, suffix_values, suffix_lengths)


def build(mesh, dims, row_chunks):
    placed = (
        P("req", "pre"),
        P(("pre", "req"), None),
        P(("pre", "req"), None),
        P("req", "pre", None),
        P("req", "pre", None),
        P("req"),
    )
    return jax.shard_map(
        functools.partial(on_device, dims, row_chunks),
        mesh=mesh, in_specs=placed, out_specs=P("req", "pre"), check_vma=False,
    )


def solution(mesh):
    return build(mesh, (8, 4, 4), 2)
```

```python
import functools
import math

import jax
import jax.numpy as jnp
from jax import lax
from jax.experimental import pallas as pl
from jax.experimental.pallas import tpu as pltpu
from jax.sharding import PartitionSpec as P

MESH = pl.DeviceIdType.MESH
DH = 128
HG = 16
F32 = jnp.float32
BF16 = jnp.bfloat16
SCALE = math.log2(math.e) / math.sqrt(DH)
NEG = -1e30


def plane_chips(nx, ny):
    def hops(o):
        return min(o[0], nx - o[0]) + min(o[1], ny - o[1])

    chips = sorted([(i, j) for i in range(nx) for j in range(ny)], key=lambda o: -hops(o))
    back = [chips.index(((-i) % nx, (-j) % ny)) for i, j in chips]
    return chips, back


def kernel(
    dims, row_chunks,
    q_ref, k_ref, v_ref, sk_ref, sv_ref, len_ref, out_ref,
    qrow, length, kb, vx, skb, svb, qy, qo, qa, ob, ib, st, ist, zo, zi, zst, zist, so, sst,
    local_sem, kvs_sem, kvr_sem, zs_sem, zr_sem, zd_sem, zo_sem, qs_sem, qr_sem, os_sem, or_sem, zz_sem, su_sem,
):
    npre, nx, ny = dims
    nreq = nx * ny * 2
    half = npre // 2
    tokens = k_ref.shape[0]
    slots = sk_ref.shape[1]
    p = lax.axis_index("pre")
    r = lax.axis_index("req")
    c = r % 2
    odd = 1 - c
    e = (p + odd) % 2
    x = r // (2 * ny)
    y = (r // 2) % ny
    chips, back = plane_chips(nx, ny)
    others = nreq - 1
    own_chip = len(chips) - 1

    def plane_mate(chip, core):
        kx, ky = chips[chip]
        return (((x + kx) % nx) * ny + (y + ky) % ny) * 2 + (c + core) % 2

    def pre_mate(k):
        return (p + k) % npre

    def columns(g):
        return pl.ds(pl.multiple_of(g * DH, DH), DH)

    def own_rows():
        return pl.ds(pl.multiple_of(c * tokens, tokens), tokens)

    def drain(ref, sem):
        pltpu.make_async_copy(ref, ref, sem).wait()

    plane = [(n, core) for n in range(len(chips)) for core in range(2)]
    barrier = pltpu.get_barrier_semaphore()
    sib = plane_mate(own_chip, 1)
    far_first = sorted(range(1, npre), key=lambda k: -min(k, npre - k))
    for k in far_first:
        pl.semaphore_signal(barrier, inc=1, device_id=(pre_mate(k), r), device_id_type=MESH)
    for n, core in plane:
        if (n, core) != (own_chip, 0):
            pl.semaphore_signal(barrier, inc=1, device_id=(p, plane_mate(n, core)), device_id_type=MESH)
    for k in far_first:
        pl.semaphore_signal(barrier, inc=1, device_id=(pre_mate(k), sib), device_id_type=MESH)

    query_copy = pltpu.make_async_copy(q_ref, qrow, local_sem.at[4])
    query_copy.start()
    length_copy = pltpu.make_async_copy(len_ref, length, local_sem.at[5])
    length_copy.start()
    for i in range(half):
        pltpu.make_async_copy(k_ref.at[:, columns(2 * i + odd)], kb.at[i, own_rows(), :], local_sem.at[0]).start()
        pltpu.make_async_copy(
            v_ref.at[:, columns(2 * i + odd)], vx.at[i, own_rows(), pl.ds(0, DH)], local_sem.at[1]
        ).start()
    suffix = [
        pltpu.make_async_copy(sk_ref.at[0], skb, local_sem.at[2]),
        pltpu.make_async_copy(sv_ref.at[0], svb, local_sem.at[3]),
    ]
    for copy in suffix:
        copy.start()

    query_copy.wait()
    tile = jnp.concatenate([qrow[:, h * DH : (h + 1) * DH].astype(F32) for h in range(HG)], axis=0)
    tile = tile.astype(BF16)

    @pl.when(e == 0)
    def _():
        qy[p // 2, c] = tile

    @pl.when(e == 1)
    def _():
        qo[p // 2] = tile


    def fill(i, carry):
        vx[i, :, DH : 2 * DH] = jnp.ones((2 * tokens, DH), BF16)
        return carry

    lax.fori_loop(0, half, fill, 0)
    pl.semaphore_wait(barrier, 2 * (npre - 1) + others)

    def line_copy(src, dst, plane_index, mate, recv):
        return pltpu.make_async_remote_copy(
            src_ref=src, dst_ref=dst, send_sem=zs_sem.at[0], recv_sem=recv,
            device_id=(plane_index, mate), device_id_type=MESH,
        )

    @pl.when(e == 0)
    def _():
        for k in far_first:
            line_copy(qy.at[p // 2, c], qy.at[p // 2, c], pre_mate(k), r, zr_sem.at[p // 2]).start()

    @pl.when(e == 1)
    def _():
        for k in far_first + [0]:
            line_copy(qo.at[p // 2], qy.at[p // 2, c], pre_mate(k), sib, zd_sem.at[p // 2]).start()
        for k in far_first:
            line_copy(qo.at[p // 2], qo.at[p // 2], pre_mate(k), r, zo_sem.at[p // 2]).start()

    def forward(h):
        g = 2 * h + odd

        @pl.when(p != g)
        def _():
            drain(qy.at[h, c], zr_sem.at[h])

        drain(qy.at[h, 1 - c], zd_sem.at[h])
        for n in range(own_chip):
            pltpu.make_async_remote_copy(
                src_ref=qy.at[h], dst_ref=qa.at[back[n], h],
                send_sem=qs_sem.at[0], recv_sem=qr_sem.at[h],
                device_id=(p, plane_mate(n, 0)), device_id_type=MESH,
            ).start()
        qa[own_chip, h] = qy[h]

    for i in range(half):
        for n, (src, dst) in enumerate(
            (
                (k_ref.at[:, columns(2 * i + 1 - odd)], kb.at[i, own_rows(), :]),
                (v_ref.at[:, columns(2 * i + 1 - odd)], vx.at[i, own_rows(), pl.ds(0, DH)]),
            )
        ):
            pltpu.make_async_remote_copy(
                src_ref=src, dst_ref=dst, send_sem=kvs_sem.at[n], recv_sem=kvr_sem.at[n, i],
                device_id=(p, sib), device_id_type=MESH,
            ).start()

    def as_row(peak, total, lanes):
        count = peak.shape[0]
        at = lax.broadcasted_iota(jnp.int32, (count, DH), 1)
        row = lax.broadcasted_iota(jnp.int32, (count, DH), 0)
        return jnp.sum(jnp.where(at == row, peak, jnp.where(at == lanes + row, total, 0.0)), axis=0, keepdims=True)

    def weigh(rows, lanes):
        table = jnp.concatenate(rows, axis=0)
        top = jnp.max(table, axis=0, keepdims=True)
        factor = jnp.exp2(table - top)
        total = jnp.sum(factor * pltpu.roll(table, DH - lanes, 1), axis=0, keepdims=True)
        pad = jnp.zeros(((-len(rows) - 2) % 8, DH), F32)
        return jnp.concatenate([factor, top, total, pad], axis=0).T

    length_copy.wait()
    for copy in suffix:
        copy.wait()
    visible = (p * slots + lax.broadcasted_iota(jnp.int32, (HG, slots), 1)) < length[0]

    def suffix_part(g, q):
        span = columns(g)
        s = lax.dot_general(q, skb[:, span], (((1,), (1,)), ((), ())), preferred_element_type=F32)
        s = jnp.where(visible, s * SCALE, NEG)
        m = jnp.max(s, axis=1, keepdims=True)
        w = jnp.where(visible, jnp.exp2(s - m), 0.0).astype(BF16)
        so[g] = jnp.dot(w, svb[:, span], preferred_element_type=F32).astype(BF16)
        sst[g] = as_row(m, jnp.sum(w.astype(F32), axis=1, keepdims=True), HG)

    for h in range(half):
        forward(h)
    for h in range(half):

        @pl.when(p != 2 * h + 1 - odd)
        def _(h=h):
            drain(qo.at[h], zo_sem.at[h])

    for h in range(half):
        suffix_part(2 * h + odd, qy[h, c])
        suffix_part(2 * h + 1 - odd, qo[h])
    for k in far_first:
        g = pre_mate(k)
        for n, (src, dst) in enumerate(((so, zi), (sst, zist))):
            pltpu.make_async_remote_copy(
                src_ref=src.at[g], dst_ref=dst.at[npre + p], send_sem=su_sem.at[n], recv_sem=su_sem.at[2 + n],
                device_id=(g, r), device_id_type=MESH,
            ).start()
    zi[npre + p] = so[p]
    zist[npre + p] = sst[p]

    keys, values = kb.at[:, pl.ds(0, tokens), :], vx.at[:, pl.ds(0, tokens), pl.ds(0, DH)]
    drain(keys, local_sem.at[0])
    drain(values, local_sem.at[1])

    chunk = nreq // row_chunks
    per = chunk // 2
    pair_lane = lax.broadcasted_iota(jnp.int32, (chunk * HG, DH), 1)
    pair_row = lax.broadcasted_iota(jnp.int32, (chunk * HG, DH), 0) % (2 * HG)

    def group_step(i, carry):
        drain(kb.at[0, pl.ds(0, tokens)], kvr_sem.at[0, i])
        drain(vx.at[0, pl.ds(0, tokens), pl.ds(0, DH)], kvr_sem.at[1, i])
        drain(qa.at[pl.ds(0, own_chip), 0], qr_sem.at[i])

        def scores(ch):
            qc = qa[pl.ds(ch * per, per), i].reshape(chunk * HG, DH)
            return lax.dot_general(qc, kb[i], (((1,), (1,)), ((), ())), preferred_element_type=F32)

        s = scores(0)
        for ch in range(row_chunks):
            after = scores(ch + 1) if ch + 1 < row_chunks else None
            m = (jnp.max(s, axis=1, keepdims=True) * SCALE).astype(BF16).astype(F32)
            w = jnp.exp2(s * SCALE - m).astype(BF16)
            o = jnp.dot(w, vx[i], preferred_element_type=F32)
            ob[i, pl.ds(ch * per, per)] = o[:, :DH].astype(BF16).reshape(per, 2, HG, DH)
            stats = jnp.where(pair_lane == pair_row, m, 0.0)
            stats = jnp.where(pair_lane == DH // 2 + pair_row, o[:, DH:], stats)
            rows = jnp.sum(stats.reshape(per, 2 * HG, DH), axis=1)
            for n in range(per):
                st[i, ch * per + n] = rows[n : n + 1]
            s = after
        for n in range(own_chip):
            for a, (src, dst) in enumerate(((ob, ib), (st, ist))):
                pltpu.make_async_remote_copy(
                    src_ref=src.at[i, n], dst_ref=dst.at[i, back[n]],
                    send_sem=os_sem.at[a], recv_sem=or_sem.at[a, i],
                    device_id=(p, plane_mate(n, 0)), device_id_type=MESH,
                ).start()
        ib[i, own_chip] = ob[i, own_chip]
        ist[i, own_chip] = st[i, own_chip]
        return carry

    lax.fori_loop(0, half, group_step, 0)

    def combine_step(i, carry):
        drain(ist.at[i, pl.ds(0, own_chip)], or_sem.at[1, i])
        columns_of = weigh([ist[i, n] for n in range(len(chips))], DH // 2)[: 2 * HG]
        drain(ib.at[i, pl.ds(0, own_chip)], or_sem.at[0, i])
        num = functools.reduce(
            jnp.add,
            [columns_of[:, n : n + 1] * ib[i, n].reshape(2 * HG, DH).astype(F32) for n in range(len(chips))],
        )
        zo[i] = num.astype(BF16).reshape(2, HG, DH)
        for core in range(2):
            part = columns_of[HG * core : HG * (core + 1)]
            zst[i, core] = as_row(part[:, len(chips) : len(chips) + 1], part[:, len(chips) + 1 : len(chips) + 2], HG)
        g = 2 * i + odd

        def send(core, mate):
            for n, (src, dst) in enumerate(((zo, zi), (zst, zist))):
                pltpu.make_async_remote_copy(
                    src_ref=src.at[i, core], dst_ref=dst.at[p], send_sem=zz_sem.at[n], recv_sem=zz_sem.at[2 + n],
                    device_id=(g, mate), device_id_type=MESH,
                ).start()

        send(1 - c, sib)

        @pl.when(g != p)
        def _():
            send(c, r)

        @pl.when(g == p)
        def _():
            zi[p] = zo[i, c]
            zist[p] = zst[i, c]

        return carry

    lax.fori_loop(0, half, combine_step, 0)

    def both_cores(array, sem):
        @pl.when(e == 0)
        def _():
            drain(array.at[pl.ds(0, npre - 1)], sem)

        @pl.when(e == 1)
        def _():
            drain(array.at[pl.ds(0, npre)], sem)

    drain(zi.at[pl.ds(0, npre - 1)], su_sem.at[2])
    drain(zist.at[pl.ds(0, npre - 1)], su_sem.at[3])
    both_cores(zist, zz_sem.at[3])
    columns_of = weigh([zist[k] for k in range(2 * npre)], HG)[:HG]
    both_cores(zi, zz_sem.at[2])
    num = functools.reduce(jnp.add, [columns_of[:, k : k + 1] * zi[k].astype(F32) for k in range(2 * npre)])
    result = (num / columns_of[:, 2 * npre + 1 : 2 * npre + 2]).astype(BF16)
    for h in range(HG):
        out_ref[:, h * DH : (h + 1) * DH] = result[h : h + 1]

    @pl.when(e == 0)
    def _():
        drain(zi.at[pl.ds(0, npre - 1)], zs_sem.at[0])

    @pl.when(e == 1)
    def _():
        drain(zi.at[pl.ds(0, 2 * npre - 1)], zs_sem.at[0])

    drain(keys, kvs_sem.at[0])
    drain(values, kvs_sem.at[1])
    drain(qa.at[pl.ds(0, own_chip)], qs_sem.at[0])
    drain(ib.at[:, pl.ds(0, own_chip)], os_sem.at[0])
    drain(ist.at[:, pl.ds(0, own_chip)], os_sem.at[1])
    drain(zi.at[pl.ds(0, npre - 1)], su_sem.at[0])
    drain(zist.at[pl.ds(0, npre - 1)], su_sem.at[1])
    both_cores(zi, zz_sem.at[0])
    both_cores(zist, zz_sem.at[1])


def on_device(dims, row_chunks, queries, prefix_keys, prefix_values, suffix_keys, suffix_values, suffix_lengths):
    npre, nx, ny = dims
    nreq = nx * ny * 2
    half = npre // 2
    tokens = prefix_keys.shape[0]
    slots = suffix_keys.shape[1]
    width = npre * DH
    vmem = pl.BlockSpec(memory_space=pltpu.VMEM)
    hbm = pl.BlockSpec(memory_space=pl.ANY)
    dma = pltpu.SemaphoreType.DMA
    return pl.pallas_call(
        functools.partial(kernel, dims, row_chunks),
        out_shape=pltpu.VMEM((1, HG * DH), BF16),
        in_specs=[hbm] * 6,
        out_specs=vmem,
        scratch_shapes=[
            pltpu.VMEM((1, HG * DH), BF16),
            pltpu.SMEM((1,), jnp.int32),
            pltpu.VMEM((half, 2 * tokens, DH), BF16),
            pltpu.VMEM((half, 2 * tokens, 2 * DH), BF16),
            pltpu.VMEM((slots, width), BF16),
            pltpu.VMEM((slots, width), BF16),
            pltpu.VMEM((half, 2, HG, DH), BF16),
            pltpu.VMEM((half, HG, DH), BF16),
            pltpu.VMEM((nreq // 2, half, 2, HG, DH), BF16),
            pltpu.VMEM((half, nreq // 2, 2, HG, DH), BF16),
            pltpu.VMEM((half, nreq // 2, 2, HG, DH), BF16),
            pltpu.VMEM((half, nreq // 2, 1, DH), F32),
            pltpu.VMEM((half, nreq // 2, 1, DH), F32),
            pltpu.VMEM((half, 2, HG, DH), BF16),
            pltpu.VMEM((2 * npre, HG, DH), BF16),
            pltpu.VMEM((half, 2, 1, DH), F32),
            pltpu.VMEM((2 * npre, 1, DH), F32),
            pltpu.VMEM((npre, HG, DH), BF16),
            pltpu.VMEM((npre, 1, DH), F32),
            dma((6,)),
            dma((2,)),
            dma((2, half)),
            dma((1,)),
            dma((half,)),
            dma((half,)),
            dma((half,)),
            dma((1,)),
            dma((half,)),
            dma((2,)),
            dma((2, half)),
            dma((4,)),
            dma((4,)),
        ],
        compiler_params=pltpu.CompilerParams(
            collective_id=0, has_side_effects=True, vmem_limit_bytes=60 * 1024 * 1024
        ),
    )(queries, prefix_keys, prefix_values, suffix_keys, suffix_values, suffix_lengths)


def build(mesh, dims, row_chunks):
    placed = (
        P("req", "pre"),
        P(("pre", "req"), None),
        P(("pre", "req"), None),
        P("req", "pre", None),
        P("req", "pre", None),
        P("req"),
    )
    return jax.shard_map(
        functools.partial(on_device, dims, row_chunks),
        mesh=mesh, in_specs=placed, out_specs=P("req", "pre"), check_vma=False,
    )


def solution(mesh):
    return build(mesh, (8, 4, 4), 2)
```

```python
import functools
import math

import jax
import jax.numpy as jnp
from jax import lax
from jax.experimental import pallas as pl
from jax.experimental.pallas import tpu as pltpu
from jax.sharding import PartitionSpec as P

MESH = pl.DeviceIdType.MESH
DH = 128
HG = 16
F32 = jnp.float32
BF16 = jnp.bfloat16
SCALE = math.log2(math.e) / math.sqrt(DH)
NEG = -1e30


def plane_chips(nx, ny):
    def hops(o):
        return min(o[0], nx - o[0]) + min(o[1], ny - o[1])

    chips = sorted([(i, j) for i in range(nx) for j in range(ny)], key=lambda o: -hops(o))
    back = [chips.index(((-i) % nx, (-j) % ny)) for i, j in chips]
    return chips, back


def kernel(
    dims, row_chunks,
    q_ref, k_ref, v_ref, sk_ref, sv_ref, len_ref, out_ref,
    qrow, length, kb, vx, skb, svb, qy, qo, qa, ob, ib, st, ist, zo, zi, zst, zist, so, sst,
    local_sem, kvs_sem, kvr_sem, zs_sem, zr_sem, zd_sem, zo_sem, qs_sem, qr_sem, os_sem, or_sem, zz_sem, su_sem,
):
    npre, nx, ny = dims
    nreq = nx * ny * 2
    half = npre // 2
    tokens = k_ref.shape[0]
    slots = sk_ref.shape[1]
    p = lax.axis_index("pre")
    r = lax.axis_index("req")
    c = r % 2
    odd = 1 - c
    e = (p + odd) % 2
    x = r // (2 * ny)
    y = (r // 2) % ny
    chips, back = plane_chips(nx, ny)
    own_chip = len(chips) - 1

    def plane_mate(chip, core):
        kx, ky = chips[chip]
        return (((x + kx) % nx) * ny + (y + ky) % ny) * 2 + (c + core) % 2

    def pre_mate(k):
        return (p + k) % npre

    def columns(g):
        return pl.ds(pl.multiple_of(g * DH, DH), DH)

    def own_rows():
        return pl.ds(pl.multiple_of(c * tokens, tokens), tokens)

    def drain(ref, sem):
        pltpu.make_async_copy(ref, ref, sem).wait()

    barrier = pltpu.get_barrier_semaphore()
    sib = plane_mate(own_chip, 1)
    far_first = sorted(range(1, npre), key=lambda k: -min(k, npre - k))
    for mate in (r, sib):
        for k in far_first:
            pl.semaphore_signal(barrier, inc=1, device_id=(pre_mate(k), mate), device_id_type=MESH)
    for n in range(own_chip):
        pl.semaphore_signal(barrier, inc=1, device_id=(p, plane_mate(n, 0)), device_id_type=MESH)
    pl.semaphore_signal(barrier, inc=1, device_id=(p, sib), device_id_type=MESH)

    query_copy = pltpu.make_async_copy(q_ref, qrow, local_sem.at[4])
    query_copy.start()
    length_copy = pltpu.make_async_copy(len_ref, length, local_sem.at[5])
    length_copy.start()
    for i in range(half):
        pltpu.make_async_copy(k_ref.at[:, columns(2 * i + odd)], kb.at[i, own_rows(), :], local_sem.at[0]).start()
        pltpu.make_async_copy(
            v_ref.at[:, columns(2 * i + odd)], vx.at[i, own_rows(), pl.ds(0, DH)], local_sem.at[1]
        ).start()
    suffix = [
        pltpu.make_async_copy(sk_ref.at[0], skb, local_sem.at[2]),
        pltpu.make_async_copy(sv_ref.at[0], svb, local_sem.at[3]),
    ]
    for copy in suffix:
        copy.start()

    query_copy.wait()
    tile = jnp.concatenate([qrow[:, h * DH : (h + 1) * DH].astype(F32) for h in range(HG)], axis=0)
    tile = tile.astype(BF16)

    @pl.when(e == 0)
    def _():
        qy[p // 2, c] = tile

    @pl.when(e == 1)
    def _():
        qo[p // 2] = tile


    def fill(i, carry):
        vx[i, :, DH : 2 * DH] = jnp.ones((2 * tokens, DH), BF16)
        return carry

    lax.fori_loop(0, half, fill, 0)
    pl.semaphore_wait(barrier, 2 * (npre - 1) + own_chip + 1)

    def line_copy(src, dst, plane_index, mate, recv):
        return pltpu.make_async_remote_copy(
            src_ref=src, dst_ref=dst, send_sem=zs_sem.at[0], recv_sem=recv,
            device_id=(plane_index, mate), device_id_type=MESH,
        )

    @pl.when(e == 0)
    def _():
        for k in far_first:
            line_copy(qy.at[p // 2, c], qy.at[p // 2, c], pre_mate(k), r, zr_sem.at[p // 2]).start()

    @pl.when(e == 1)
    def _():
        for k in far_first + [0]:
            line_copy(qo.at[p // 2], qy.at[p // 2, c], pre_mate(k), sib, zd_sem.at[p // 2]).start()
        for k in far_first:
            line_copy(qo.at[p // 2], qo.at[p // 2], pre_mate(k), r, zo_sem.at[p // 2]).start()

    def forward(h):
        g = 2 * h + odd

        @pl.when(p != g)
        def _():
            drain(qy.at[h, c], zr_sem.at[h])

        drain(qy.at[h, 1 - c], zd_sem.at[h])
        for n in range(own_chip):
            pltpu.make_async_remote_copy(
                src_ref=qy.at[h], dst_ref=qa.at[back[n], h],
                send_sem=qs_sem.at[0], recv_sem=qr_sem.at[h],
                device_id=(p, plane_mate(n, 0)), device_id_type=MESH,
            ).start()
        qa[own_chip, h] = qy[h]

    for i in range(half):
        for n, (src, dst) in enumerate(
            (
                (k_ref.at[:, columns(2 * i + 1 - odd)], kb.at[i, own_rows(), :]),
                (v_ref.at[:, columns(2 * i + 1 - odd)], vx.at[i, own_rows(), pl.ds(0, DH)]),
            )
        ):
            pltpu.make_async_remote_copy(
                src_ref=src, dst_ref=dst, send_sem=kvs_sem.at[n], recv_sem=kvr_sem.at[n, i],
                device_id=(p, sib), device_id_type=MESH,
            ).start()

    def as_row(peak, total, lanes):
        count = peak.shape[0]
        at = lax.broadcasted_iota(jnp.int32, (count, DH), 1)
        row = lax.broadcasted_iota(jnp.int32, (count, DH), 0)
        return jnp.sum(jnp.where(at == row, peak, jnp.where(at == lanes + row, total, 0.0)), axis=0, keepdims=True)

    def weigh(rows, lanes):
        table = jnp.concatenate(rows, axis=0)
        top = jnp.max(table, axis=0, keepdims=True)
        factor = jnp.exp2(table - top)
        total = jnp.sum(factor * pltpu.roll(table, DH - lanes, 1), axis=0, keepdims=True)
        pad = jnp.zeros(((-len(rows) - 2) % 8, DH), F32)
        return jnp.concatenate([factor, top, total, pad], axis=0).T

    length_copy.wait()
    for copy in suffix:
        copy.wait()
    visible = (p * slots + lax.broadcasted_iota(jnp.int32, (HG, slots), 1)) < length[0]

    def suffix_part(g, q):
        span = columns(g)
        s = lax.dot_general(q, skb[:, span], (((1,), (1,)), ((), ())), preferred_element_type=F32)
        s = jnp.where(visible, s * SCALE, NEG)
        m = jnp.max(s, axis=1, keepdims=True)
        w = jnp.where(visible, jnp.exp2(s - m), 0.0).astype(BF16)
        so[g] = jnp.dot(w, svb[:, span], preferred_element_type=F32).astype(BF16)
        sst[g] = as_row(m, jnp.sum(w.astype(F32), axis=1, keepdims=True), HG)

    for h in range(half):
        forward(h)
    for h in range(half):

        @pl.when(p != 2 * h + 1 - odd)
        def _(h=h):
            drain(qo.at[h], zo_sem.at[h])

    for h in range(half):
        suffix_part(2 * h + odd, qy[h, c])
        suffix_part(2 * h + 1 - odd, qo[h])
    for k in far_first:
        g = pre_mate(k)
        for n, (src, dst) in enumerate(((so, zi), (sst, zist))):
            pltpu.make_async_remote_copy(
                src_ref=src.at[g], dst_ref=dst.at[npre + p], send_sem=su_sem.at[n], recv_sem=su_sem.at[2 + n],
                device_id=(g, r), device_id_type=MESH,
            ).start()
    zi[npre + p] = so[p]
    zist[npre + p] = sst[p]

    keys, values = kb.at[:, pl.ds(0, tokens), :], vx.at[:, pl.ds(0, tokens), pl.ds(0, DH)]
    drain(keys, local_sem.at[0])
    drain(values, local_sem.at[1])

    chunk = nreq // row_chunks
    per = chunk // 2
    pair_lane = lax.broadcasted_iota(jnp.int32, (chunk * HG, DH), 1)
    pair_row = lax.broadcasted_iota(jnp.int32, (chunk * HG, DH), 0) % (2 * HG)

    def group_step(i, carry):
        drain(kb.at[0, pl.ds(0, tokens)], kvr_sem.at[0, i])
        drain(vx.at[0, pl.ds(0, tokens), pl.ds(0, DH)], kvr_sem.at[1, i])
        drain(qa.at[pl.ds(0, own_chip), 0], qr_sem.at[i])

        def scores(ch):
            qc = qa[pl.ds(ch * per, per), i].reshape(chunk * HG, DH)
            return lax.dot_general(qc, kb[i], (((1,), (1,)), ((), ())), preferred_element_type=F32)

        s = scores(0)
        for ch in range(row_chunks):
            after = scores(ch + 1) if ch + 1 < row_chunks else None
            m = (jnp.max(s, axis=1, keepdims=True) * SCALE).astype(BF16).astype(F32)
            w = jnp.exp2(s * SCALE - m).astype(BF16)
            o = jnp.dot(w, vx[i], preferred_element_type=F32)
            ob[i, pl.ds(ch * per, per)] = o[:, :DH].astype(BF16).reshape(per, 2, HG, DH)
            stats = jnp.where(pair_lane == pair_row, m, 0.0)
            stats = jnp.where(pair_lane == DH // 2 + pair_row, o[:, DH:], stats)
            rows = jnp.sum(stats.reshape(per, 2 * HG, DH), axis=1)
            for n in range(per):
                st[i, ch * per + n] = rows[n : n + 1]
            s = after
        for n in range(own_chip):
            for a, (src, dst) in enumerate(((ob, ib), (st, ist))):
                pltpu.make_async_remote_copy(
                    src_ref=src.at[i, n], dst_ref=dst.at[i, back[n]],
                    send_sem=os_sem.at[a], recv_sem=or_sem.at[a, i],
                    device_id=(p, plane_mate(n, 0)), device_id_type=MESH,
                ).start()
        ib[i, own_chip] = ob[i, own_chip]
        ist[i, own_chip] = st[i, own_chip]
        return carry

    lax.fori_loop(0, half, group_step, 0)

    def combine_step(i, carry):
        drain(ist.at[i, pl.ds(0, own_chip)], or_sem.at[1, i])
        columns_of = weigh([ist[i, n] for n in range(len(chips))], DH // 2)[: 2 * HG]
        drain(ib.at[i, pl.ds(0, own_chip)], or_sem.at[0, i])
        num = functools.reduce(
            jnp.add,
            [columns_of[:, n : n + 1] * ib[i, n].reshape(2 * HG, DH).astype(F32) for n in range(len(chips))],
        )
        zo[i] = num.astype(BF16).reshape(2, HG, DH)
        for core in range(2):
            part = columns_of[HG * core : HG * (core + 1)]
            zst[i, core] = as_row(part[:, len(chips) : len(chips) + 1], part[:, len(chips) + 1 : len(chips) + 2], HG)
        g = 2 * i + odd

        def send(core, mate):
            for n, (src, dst) in enumerate(((zo, zi), (zst, zist))):
                pltpu.make_async_remote_copy(
                    src_ref=src.at[i, core], dst_ref=dst.at[p], send_sem=zz_sem.at[n], recv_sem=zz_sem.at[2 + n],
                    device_id=(g, mate), device_id_type=MESH,
                ).start()

        send(1 - c, sib)

        @pl.when(g != p)
        def _():
            send(c, r)

        @pl.when(g == p)
        def _():
            zi[p] = zo[i, c]
            zist[p] = zst[i, c]

        return carry

    lax.fori_loop(0, half, combine_step, 0)

    def both_cores(array, sem):
        @pl.when(e == 0)
        def _():
            drain(array.at[pl.ds(0, npre - 1)], sem)

        @pl.when(e == 1)
        def _():
            drain(array.at[pl.ds(0, npre)], sem)

    @pl.when(e == 0)
    def _():
        drain(zi.at[pl.ds(0, npre - 1)], zs_sem.at[0])

    @pl.when(e == 1)
    def _():
        drain(zi.at[pl.ds(0, 2 * npre - 1)], zs_sem.at[0])

    drain(keys, kvs_sem.at[0])
    drain(values, kvs_sem.at[1])
    drain(qa.at[pl.ds(0, own_chip)], qs_sem.at[0])
    drain(ib.at[:, pl.ds(0, own_chip)], os_sem.at[0])
    drain(ist.at[:, pl.ds(0, own_chip)], os_sem.at[1])
    drain(zi.at[pl.ds(0, npre - 1)], su_sem.at[0])
    drain(zist.at[pl.ds(0, npre - 1)], su_sem.at[1])
    drain(zi.at[pl.ds(0, npre - 1)], su_sem.at[2])
    drain(zist.at[pl.ds(0, npre - 1)], su_sem.at[3])
    both_cores(zist, zz_sem.at[3])
    columns_of = weigh([zist[k] for k in range(2 * npre)], HG)[:HG]
    both_cores(zi, zz_sem.at[2])
    num = functools.reduce(jnp.add, [columns_of[:, k : k + 1] * zi[k].astype(F32) for k in range(2 * npre)])
    result = (num / columns_of[:, 2 * npre + 1 : 2 * npre + 2]).astype(BF16)
    for h in range(HG):
        out_ref[:, h * DH : (h + 1) * DH] = result[h : h + 1]

    both_cores(zi, zz_sem.at[0])
    both_cores(zist, zz_sem.at[1])


def on_device(dims, row_chunks, queries, prefix_keys, prefix_values, suffix_keys, suffix_values, suffix_lengths):
    npre, nx, ny = dims
    nreq = nx * ny * 2
    half = npre // 2
    tokens = prefix_keys.shape[0]
    slots = suffix_keys.shape[1]
    width = npre * DH
    vmem = pl.BlockSpec(memory_space=pltpu.VMEM)
    hbm = pl.BlockSpec(memory_space=pl.ANY)
    dma = pltpu.SemaphoreType.DMA
    return pl.pallas_call(
        functools.partial(kernel, dims, row_chunks),
        out_shape=pltpu.VMEM((1, HG * DH), BF16),
        in_specs=[hbm] * 6,
        out_specs=vmem,
        scratch_shapes=[
            pltpu.VMEM((1, HG * DH), BF16),
            pltpu.SMEM((1,), jnp.int32),
            pltpu.VMEM((half, 2 * tokens, DH), BF16),
            pltpu.VMEM((half, 2 * tokens, 2 * DH), BF16),
            pltpu.VMEM((slots, width), BF16),
            pltpu.VMEM((slots, width), BF16),
            pltpu.VMEM((half, 2, HG, DH), BF16),
            pltpu.VMEM((half, HG, DH), BF16),
            pltpu.VMEM((nreq // 2, half, 2, HG, DH), BF16),
            pltpu.VMEM((half, nreq // 2, 2, HG, DH), BF16),
            pltpu.VMEM((half, nreq // 2, 2, HG, DH), BF16),
            pltpu.VMEM((half, nreq // 2, 1, DH), F32),
            pltpu.VMEM((half, nreq // 2, 1, DH), F32),
            pltpu.VMEM((half, 2, HG, DH), BF16),
            pltpu.VMEM((2 * npre, HG, DH), BF16),
            pltpu.VMEM((half, 2, 1, DH), F32),
            pltpu.VMEM((2 * npre, 1, DH), F32),
            pltpu.VMEM((npre, HG, DH), BF16),
            pltpu.VMEM((npre, 1, DH), F32),
            dma((6,)),
            dma((2,)),
            dma((2, half)),
            dma((1,)),
            dma((half,)),
            dma((half,)),
            dma((half,)),
            dma((1,)),
            dma((half,)),
            dma((2,)),
            dma((2, half)),
            dma((4,)),
            dma((4,)),
        ],
        compiler_params=pltpu.CompilerParams(
            collective_id=0, has_side_effects=True, vmem_limit_bytes=60 * 1024 * 1024
        ),
    )(queries, prefix_keys, prefix_values, suffix_keys, suffix_values, suffix_lengths)


def build(mesh, dims, row_chunks):
    placed = (
        P("req", "pre"),
        P(("pre", "req"), None),
        P(("pre", "req"), None),
        P("req", "pre", None),
        P("req", "pre", None),
        P("req"),
    )
    return jax.shard_map(
        functools.partial(on_device, dims, row_chunks),
        mesh=mesh, in_specs=placed, out_specs=P("req", "pre"), check_vma=False,
    )


def solution(mesh):
    return build(mesh, (8, 4, 4), 2)
```

```python
import functools
import math

import jax
import jax.numpy as jnp
from jax import lax
from jax.experimental import pallas as pl
from jax.experimental.pallas import tpu as pltpu
from jax.sharding import PartitionSpec as P

MESH = pl.DeviceIdType.MESH
DH = 128
HG = 16
F32 = jnp.float32
BF16 = jnp.bfloat16
SCALE = math.log2(math.e) / math.sqrt(DH)
NEG = -1e30


def plane_chips(nx, ny):
    def hops(o):
        return min(o[0], nx - o[0]) + min(o[1], ny - o[1])

    chips = sorted([(i, j) for i in range(nx) for j in range(ny)], key=lambda o: -hops(o))
    back = [chips.index(((-i) % nx, (-j) % ny)) for i, j in chips]
    return chips, back


def kernel(
    dims, row_chunks,
    q_ref, k_ref, v_ref, sk_ref, sv_ref, len_ref, out_ref,
    qrow, length, kb, vx, skb, svb, qy, qo, qa, ob, ib, st, ist, zo, zi, zst, zist, so, sst,
    local_sem, kvs_sem, kvr_sem, zs_sem, zr_sem, zd_sem, zo_sem, qs_sem, qr_sem, os_sem, or_sem, zz_sem, su_sem,
):
    npre, nx, ny = dims
    nreq = nx * ny * 2
    half = npre // 2
    tokens = k_ref.shape[0]
    slots = sk_ref.shape[1]
    p = lax.axis_index("pre")
    r = lax.axis_index("req")
    c = r % 2
    odd = 1 - c
    e = (p + odd) % 2
    x = r // (2 * ny)
    y = (r // 2) % ny
    chips, back = plane_chips(nx, ny)
    own_chip = len(chips) - 1

    def plane_mate(chip, core):
        kx, ky = chips[chip]
        return (((x + kx) % nx) * ny + (y + ky) % ny) * 2 + (c + core) % 2

    def pre_mate(k):
        return (p + k) % npre

    def columns(g):
        return pl.ds(pl.multiple_of(g * DH, DH), DH)

    def own_rows():
        return pl.ds(pl.multiple_of(c * tokens, tokens), tokens)

    def drain(ref, sem):
        pltpu.make_async_copy(ref, ref, sem).wait()

    barrier = pltpu.get_barrier_semaphore()
    sib = plane_mate(own_chip, 1)
    far_first = sorted(range(1, npre), key=lambda k: -min(k, npre - k))
    for mate in (r, sib):
        for k in far_first:
            pl.semaphore_signal(barrier, inc=1, device_id=(pre_mate(k), mate), device_id_type=MESH)
    for n in range(own_chip):
        pl.semaphore_signal(barrier, inc=1, device_id=(p, plane_mate(n, 0)), device_id_type=MESH)
    pl.semaphore_signal(barrier, inc=1, device_id=(p, sib), device_id_type=MESH)

    query_copy = pltpu.make_async_copy(q_ref, qrow, local_sem.at[4])
    query_copy.start()
    length_copy = pltpu.make_async_copy(len_ref, length, local_sem.at[5])
    length_copy.start()
    for i in range(half):
        pltpu.make_async_copy(k_ref.at[:, columns(2 * i + odd)], kb.at[i, own_rows(), :], local_sem.at[0]).start()
        pltpu.make_async_copy(
            v_ref.at[:, columns(2 * i + odd)], vx.at[i, own_rows(), pl.ds(0, DH)], local_sem.at[1]
        ).start()
    suffix = [
        pltpu.make_async_copy(sk_ref.at[0], skb, local_sem.at[2]),
        pltpu.make_async_copy(sv_ref.at[0], svb, local_sem.at[3]),
    ]
    for copy in suffix:
        copy.start()

    query_copy.wait()
    tile = jnp.concatenate([qrow[:, h * DH : (h + 1) * DH].astype(F32) for h in range(HG)], axis=0)
    tile = tile.astype(BF16)

    @pl.when(e == 0)
    def _():
        qy[p // 2, c] = tile

    @pl.when(e == 1)
    def _():
        qo[p // 2] = tile


    def fill(i, carry):
        vx[i, :, DH : 2 * DH] = jnp.ones((2 * tokens, DH), BF16)
        return carry

    lax.fori_loop(0, half, fill, 0)
    pl.semaphore_wait(barrier, 2 * (npre - 1) + own_chip + 1)

    def line_copy(src, dst, plane_index, mate, recv):
        return pltpu.make_async_remote_copy(
            src_ref=src, dst_ref=dst, send_sem=zs_sem.at[0], recv_sem=recv,
            device_id=(plane_index, mate), device_id_type=MESH,
        )

    @pl.when(e == 0)
    def _():
        for k in far_first:
            line_copy(qy.at[p // 2, c], qy.at[p // 2, c], pre_mate(k), r, zr_sem.at[p // 2]).start()

    @pl.when(e == 1)
    def _():
        for k in far_first + [0]:
            line_copy(qo.at[p // 2], qy.at[p // 2, c], pre_mate(k), sib, zd_sem.at[p // 2]).start()
        for k in far_first:
            line_copy(qo.at[p // 2], qo.at[p // 2], pre_mate(k), r, zo_sem.at[p // 2]).start()

    def forward(h):
        g = 2 * h + odd

        @pl.when(p != g)
        def _():
            drain(qy.at[h, c], zr_sem.at[h])

        drain(qy.at[h, 1 - c], zd_sem.at[h])
        for n in range(own_chip):
            pltpu.make_async_remote_copy(
                src_ref=qy.at[h], dst_ref=qa.at[back[n], h],
                send_sem=qs_sem.at[0], recv_sem=qr_sem.at[h],
                device_id=(p, plane_mate(n, 0)), device_id_type=MESH,
            ).start()
        qa[own_chip, h] = qy[h]

    for i in range(half):
        for n, (src, dst) in enumerate(
            (
                (k_ref.at[:, columns(2 * i + 1 - odd)], kb.at[i, own_rows(), :]),
                (v_ref.at[:, columns(2 * i + 1 - odd)], vx.at[i, own_rows(), pl.ds(0, DH)]),
            )
        ):
            pltpu.make_async_remote_copy(
                src_ref=src, dst_ref=dst, send_sem=kvs_sem.at[n], recv_sem=kvr_sem.at[n, i],
                device_id=(p, sib), device_id_type=MESH,
            ).start()

    def as_row(peak, total, lanes):
        count = peak.shape[0]
        at = lax.broadcasted_iota(jnp.int32, (count, DH), 1)
        row = lax.broadcasted_iota(jnp.int32, (count, DH), 0)
        return jnp.sum(jnp.where(at == row, peak, jnp.where(at == lanes + row, total, 0.0)), axis=0, keepdims=True)

    def weigh(rows, lanes):
        table = jnp.concatenate(rows, axis=0)
        top = jnp.max(table, axis=0, keepdims=True)
        factor = jnp.exp2(table - top)
        total = jnp.sum(factor * pltpu.roll(table, DH - lanes, 1), axis=0, keepdims=True)
        pad = jnp.zeros(((-len(rows) - 2) % 8, DH), F32)
        return jnp.concatenate([factor, top, total, pad], axis=0).T

    length_copy.wait()
    for copy in suffix:
        copy.wait()
    visible = (p * slots + lax.broadcasted_iota(jnp.int32, (HG, slots), 1)) < length[0]

    def suffix_part(g, q):
        span = columns(g)
        s = lax.dot_general(q, skb[:, span], (((1,), (1,)), ((), ())), preferred_element_type=F32)
        s = jnp.where(visible, s * SCALE, NEG)
        m = jnp.max(s, axis=1, keepdims=True)
        w = jnp.where(visible, jnp.exp2(s - m), 0.0).astype(BF16)
        so[g] = jnp.dot(w, svb[:, span], preferred_element_type=F32).astype(BF16)
        sst[g] = as_row(m, jnp.sum(w.astype(F32), axis=1, keepdims=True), HG)

    for h in range(half):
        forward(h)
    for h in range(half):

        @pl.when(p != 2 * h + 1 - odd)
        def _(h=h):
            drain(qo.at[h], zo_sem.at[h])

    for h in range(half):
        suffix_part(2 * h + odd, qy[h, c])
        suffix_part(2 * h + 1 - odd, qo[h])
    for k in far_first:
        g = pre_mate(k)
        for n, (src, dst) in enumerate(((so, zi), (sst, zist))):
            pltpu.make_async_remote_copy(
                src_ref=src.at[g], dst_ref=dst.at[npre + p], send_sem=su_sem.at[n], recv_sem=su_sem.at[2 + n],
                device_id=(g, r), device_id_type=MESH,
            ).start()
    zi[npre + p] = so[p]
    zist[npre + p] = sst[p]

    keys, values = kb.at[:, pl.ds(0, tokens), :], vx.at[:, pl.ds(0, tokens), pl.ds(0, DH)]
    drain(keys, local_sem.at[0])
    drain(values, local_sem.at[1])

    chunk = nreq // row_chunks
    per = chunk // 2
    pair_lane = lax.broadcasted_iota(jnp.int32, (chunk * HG, DH), 1)
    pair_row = lax.broadcasted_iota(jnp.int32, (chunk * HG, DH), 0) % (2 * HG)

    def group_step(i, carry):
        drain(kb.at[0, pl.ds(0, tokens)], kvr_sem.at[0, i])
        drain(vx.at[0, pl.ds(0, tokens), pl.ds(0, DH)], kvr_sem.at[1, i])
        drain(qa.at[pl.ds(0, own_chip), 0], qr_sem.at[i])

        def scores(ch):
            qc = qa[pl.ds(ch * per, per), i].reshape(chunk * HG, DH)
            return lax.dot_general(qc, kb[i], (((1,), (1,)), ((), ())), preferred_element_type=F32)

        s = scores(0)
        for ch in range(row_chunks):
            after = scores(ch + 1) if ch + 1 < row_chunks else None
            m = (jnp.max(s, axis=1, keepdims=True) * SCALE).astype(BF16).astype(F32)
            w = jnp.exp2(s * SCALE - m).astype(BF16)
            o = jnp.dot(w, vx[i], preferred_element_type=F32)
            ob[i, pl.ds(ch * per, per)] = o[:, :DH].astype(BF16).reshape(per, 2, HG, DH)
            stats = jnp.where(pair_lane == pair_row, m, 0.0)
            stats = jnp.where(pair_lane == DH // 2 + pair_row, o[:, DH:], stats)
            rows = jnp.sum(stats.reshape(per, 2 * HG, DH), axis=1)
            for n in range(per):
                st[i, ch * per + n] = rows[n : n + 1]
            s = after
        for a, (src, dst) in ((1, (st, ist)), (0, (ob, ib))):
            for n in range(own_chip):
                pltpu.make_async_remote_copy(
                    src_ref=src.at[i, n], dst_ref=dst.at[i, back[n]],
                    send_sem=os_sem.at[a], recv_sem=or_sem.at[a, i],
                    device_id=(p, plane_mate(n, 0)), device_id_type=MESH,
                ).start()
        ib[i, own_chip] = ob[i, own_chip]
        ist[i, own_chip] = st[i, own_chip]
        return carry

    lax.fori_loop(0, half, group_step, 0)

    def combine_step(i, carry):
        drain(ist.at[i, pl.ds(0, own_chip)], or_sem.at[1, i])
        columns_of = weigh([ist[i, n] for n in range(len(chips))], DH // 2)[: 2 * HG]
        for core in range(2):
            part = columns_of[HG * core : HG * (core + 1)]
            zst[i, core] = as_row(part[:, len(chips) : len(chips) + 1], part[:, len(chips) + 1 : len(chips) + 2], HG)
        g = 2 * i + odd

        def send(src, dst, n):
            for core, mate in ((c, r), (1 - c, sib)):
                copy = pltpu.make_async_remote_copy(
                    src_ref=src.at[i, core], dst_ref=dst.at[p], send_sem=zz_sem.at[n], recv_sem=zz_sem.at[2 + n],
                    device_id=(g, mate), device_id_type=MESH,
                )
                if mate is sib:
                    copy.start()
                else:
                    pl.when(g != p)(copy.start)

        send(zst, zist, 1)
        drain(ib.at[i, pl.ds(0, own_chip)], or_sem.at[0, i])
        num = functools.reduce(
            jnp.add,
            [columns_of[:, n : n + 1] * ib[i, n].reshape(2 * HG, DH).astype(F32) for n in range(len(chips))],
        )
        zo[i] = num.astype(BF16).reshape(2, HG, DH)
        send(zo, zi, 0)

        @pl.when(g == p)
        def _():
            zi[p] = zo[i, c]
            zist[p] = zst[i, c]

        return carry

    lax.fori_loop(0, half, combine_step, 0)

    def both_cores(array, sem):
        @pl.when(e == 0)
        def _():
            drain(array.at[pl.ds(0, npre - 1)], sem)

        @pl.when(e == 1)
        def _():
            drain(array.at[pl.ds(0, npre)], sem)

    @pl.when(e == 0)
    def _():
        drain(zi.at[pl.ds(0, npre - 1)], zs_sem.at[0])

    @pl.when(e == 1)
    def _():
        drain(zi.at[pl.ds(0, 2 * npre - 1)], zs_sem.at[0])

    drain(keys, kvs_sem.at[0])
    drain(values, kvs_sem.at[1])
    drain(qa.at[pl.ds(0, own_chip)], qs_sem.at[0])
    drain(ib.at[:, pl.ds(0, own_chip)], os_sem.at[0])
    drain(ist.at[:, pl.ds(0, own_chip)], os_sem.at[1])
    drain(zi.at[pl.ds(0, npre - 1)], su_sem.at[0])
    drain(zist.at[pl.ds(0, npre - 1)], su_sem.at[1])
    drain(zi.at[pl.ds(0, npre - 1)], su_sem.at[2])
    drain(zist.at[pl.ds(0, npre - 1)], su_sem.at[3])
    both_cores(zist, zz_sem.at[3])
    columns_of = weigh([zist[k] for k in range(2 * npre)], HG)[:HG]
    both_cores(zi, zz_sem.at[2])
    num = functools.reduce(jnp.add, [columns_of[:, k : k + 1] * zi[k].astype(F32) for k in range(2 * npre)])
    result = (num / columns_of[:, 2 * npre + 1 : 2 * npre + 2]).astype(BF16)
    for h in range(HG):
        out_ref[:, h * DH : (h + 1) * DH] = result[h : h + 1]

    both_cores(zi, zz_sem.at[0])
    both_cores(zist, zz_sem.at[1])


def on_device(dims, row_chunks, queries, prefix_keys, prefix_values, suffix_keys, suffix_values, suffix_lengths):
    npre, nx, ny = dims
    nreq = nx * ny * 2
    half = npre // 2
    tokens = prefix_keys.shape[0]
    slots = suffix_keys.shape[1]
    width = npre * DH
    vmem = pl.BlockSpec(memory_space=pltpu.VMEM)
    hbm = pl.BlockSpec(memory_space=pl.ANY)
    dma = pltpu.SemaphoreType.DMA
    return pl.pallas_call(
        functools.partial(kernel, dims, row_chunks),
        out_shape=pltpu.VMEM((1, HG * DH), BF16),
        in_specs=[hbm] * 6,
        out_specs=vmem,
        scratch_shapes=[
            pltpu.VMEM((1, HG * DH), BF16),
            pltpu.SMEM((1,), jnp.int32),
            pltpu.VMEM((half, 2 * tokens, DH), BF16),
            pltpu.VMEM((half, 2 * tokens, 2 * DH), BF16),
            pltpu.VMEM((slots, width), BF16),
            pltpu.VMEM((slots, width), BF16),
            pltpu.VMEM((half, 2, HG, DH), BF16),
            pltpu.VMEM((half, HG, DH), BF16),
            pltpu.VMEM((nreq // 2, half, 2, HG, DH), BF16),
            pltpu.VMEM((half, nreq // 2, 2, HG, DH), BF16),
            pltpu.VMEM((half, nreq // 2, 2, HG, DH), BF16),
            pltpu.VMEM((half, nreq // 2, 1, DH), F32),
            pltpu.VMEM((half, nreq // 2, 1, DH), F32),
            pltpu.VMEM((half, 2, HG, DH), BF16),
            pltpu.VMEM((2 * npre, HG, DH), BF16),
            pltpu.VMEM((half, 2, 1, DH), F32),
            pltpu.VMEM((2 * npre, 1, DH), F32),
            pltpu.VMEM((npre, HG, DH), BF16),
            pltpu.VMEM((npre, 1, DH), F32),
            dma((6,)),
            dma((2,)),
            dma((2, half)),
            dma((1,)),
            dma((half,)),
            dma((half,)),
            dma((half,)),
            dma((1,)),
            dma((half,)),
            dma((2,)),
            dma((2, half)),
            dma((4,)),
            dma((4,)),
        ],
        compiler_params=pltpu.CompilerParams(
            collective_id=0, has_side_effects=True, vmem_limit_bytes=60 * 1024 * 1024
        ),
    )(queries, prefix_keys, prefix_values, suffix_keys, suffix_values, suffix_lengths)


def build(mesh, dims, row_chunks):
    placed = (
        P("req", "pre"),
        P(("pre", "req"), None),
        P(("pre", "req"), None),
        P("req", "pre", None),
        P("req", "pre", None),
        P("req"),
    )
    return jax.shard_map(
        functools.partial(on_device, dims, row_chunks),
        mesh=mesh, in_specs=placed, out_specs=P("req", "pre"), check_vma=False,
    )


def solution(mesh):
    return build(mesh, (8, 4, 4), 2)
```
